32 devices in a mesh: lon: 16 (over z, x, core), lat: 2 (over y).
Axes of the slice: x: 2, y: 2, z: 4, core: 2. Of those that a mesh axis runs over, the one named last changes fastest.
Arguments:
- thermal_anomaly: float32 [75, 32, 256], P(None, 'lon', 'lat'), may hold values from -6 to 6
- saltiness_anomaly: float32 [75, 32, 256], P(None, 'lon', 'lat'), may hold values from -6 to 6
- zonal_flow: float32 [75, 32, 256], P(None, 'lon', 'lat'), may hold values from -3 to 3
- meridional_flow: float32 [75, 32, 256], P(None, 'lon', 'lat'), may hold values from -3 to 3
- flooded_layer_number: int32 [32, 256], P('lon', 'lat'), may hold values from 0 to 75
- sideways_diffusion: float32 [32, 256], P('lon', 'lat'), may hold values from 0.2 to 4
- ambient_diffusion: float32 [32, 256], P('lon', 'lat'), may hold values from 0.1 to 10
Outputs:
- temp_next: float32 [75, 32, 256], P(None, 'lon', 'lat')
- salt_next: float32 [75, 32, 256], P(None, 'lon', 'lat')
- u_next: float32 [75, 32, 256], P(None, 'lon', 'lat')
- v_next: float32 [75, 32, 256], P(None, 'lon', 'lat')
The draws below stay inside these ranges and needn't reach their ends.
Inputs may be any that keep to these rules, and one draw needn't show every extreme that they name: flooded_layer_number counts wet levels from the top; 0 marks land.
All inputs are finite; a program needn't handle non-finite values.
Results may differ from the reference program's by a relative error of at most 0.0003.
Values sent between devices are 32-bit elements; how exact they have to be, the bound alone decides.
No kernel may reach another device: no remote copies, remote signals or barrier semaphores. Data moves between devices by JAX's collectives and lax.ppermute only.
A program may use at most 64 MiB of HBM per device.

```python
import math
import jax
import jax.numpy as jnp

VERTICAL_LAYERS = 75
SUBSTEPS = 2
FOLD_OFFSET = 1
ZONAL_POINTS = 32
MERIDIAN_POINTS = 256


def with_ends(drawn, rng, smallest, top_value):
    shape = drawn.shape
    spot = [jax.random.randint(jax.random.fold_in(rng, axis), (), 0, shape[axis]) for axis in range(len(shape))]
    drawn = drawn.at[tuple(spot)].set(smallest)
    longest = shape.index(max(shape))
    spot[longest] = (spot[longest] + 1) % shape[longest]
    return drawn.at[tuple(spot)].set(top_value)


def shard_levels(key, extent, pieces, low, largest):
    level, own = 1.0, jax.random.fold_in(key, 6)
    for axis_at, parts in pieces:
        heights = jnp.exp(jax.random.uniform(jax.random.fold_in(own, axis_at), (parts,), jnp.float32, low / len(pieces), largest / len(pieces)))
        level = level * jnp.repeat(heights, extent[axis_at] // parts).reshape([-1 if axis == axis_at else 1 for axis in range(len(extent))])
    return level


def centred(rng, shape, deviation, reach, split=(), held_as=jnp.bfloat16):
    loudness = shard_levels(rng, shape, split, -0.22, 0.18) if split else 1.0
    values = jax.random.normal(rng, shape, jnp.float32) * deviation * loudness
    return jnp.minimum(jnp.maximum(values, -reach), reach).astype(held_as)


def setup_inputs(seed: int = 0) -> dict:
    keys = jax.random.split(jax.random.key(seed), 8)
    return {
        "thermal_anomaly": centred(keys[0], (VERTICAL_LAYERS, ZONAL_POINTS, MERIDIAN_POINTS), 1.0, 6.0, ((1, 16), (2, 2)), jnp.float32),
        "saltiness_anomaly": centred(keys[1], (VERTICAL_LAYERS, ZONAL_POINTS, MERIDIAN_POINTS), 1.0, 6.0, ((1, 16), (2, 2)), jnp.float32),
        "zonal_flow": centred(keys[2], (VERTICAL_LAYERS, ZONAL_POINTS, MERIDIAN_POINTS), 0.5, 3.0, ((1, 16), (2, 2)), jnp.float32),
        "meridional_flow": centred(keys[3], (VERTICAL_LAYERS, ZONAL_POINTS, MERIDIAN_POINTS), 0.5, 3.0, ((1, 16), (2, 2)), jnp.float32),
        "flooded_layer_number": with_ends(jax.random.randint(keys[4], (ZONAL_POINTS, MERIDIAN_POINTS), 0, VERTICAL_LAYERS + 1), jax.random.fold_in(keys[4], 1), 0, VERTICAL_LAYERS).astype(jnp.int32),
        "sideways_diffusion": jnp.clip(jnp.exp(math.log(4.0) - 2.9957323 * jax.random.uniform(keys[5], (ZONAL_POINTS, MERIDIAN_POINTS), jnp.float32) ** shard_levels(keys[5], (ZONAL_POINTS, MERIDIAN_POINTS), ((0, 16), (1, 2)), -0.2, 0.2)), 0.2, 4.0),
        "ambient_diffusion": jnp.clip(jnp.exp(math.log(10.0) - 4.6051702 * jax.random.uniform(keys[6], (ZONAL_POINTS, MERIDIAN_POINTS), jnp.float32) ** shard_levels(keys[6], (ZONAL_POINTS, MERIDIAN_POINTS), ((0, 16), (1, 2)), -0.2, 0.2)), 0.1, 10.0),
    }


dt_step = 0.05


def density(temp_field, salt_field):
    return 0.8 * salt_field - 0.2 * temp_field - 0.05 * temp_field * temp_field + 0.03 * temp_field * salt_field


def coriolis_rows(first_row, row_total, total_rows):
    row_index = first_row + jnp.arange(row_total, dtype=jnp.int32)
    mirrored = jnp.where(row_index >= total_rows, 2 * total_rows - 1 - row_index, row_index)
    return 0.2 + mirrored.astype(jnp.float32) / total_rows


def centre(array):
    return array[..., 1:-1, 1:-1]


def to_east(array):
    return array[..., 2:, 1:-1]


def to_west(array):
    return array[..., :-2, 1:-1]


def to_north(array):
    return array[..., 1:-1, 2:]


def to_south(array):
    return array[..., 1:-1, :-2]


def advance(padded, planet):
    layer_total = (padded.shape[0] - 2) // 4
    marine_state = padded[:4 * layer_total].reshape(4, layer_total, padded.shape[1], padded.shape[2])
    bottom = padded[4 * layer_total]
    lateral = padded[4 * layer_total + 1]
    level_index = jnp.arange(layer_total, dtype=jnp.float32)[:, None, None]
    wet_mask = (level_index < bottom[None]).astype(jnp.float32)
    pressure = 0.5 * jnp.cumsum(density(marine_state[0], marine_state[1]), axis=0)
    wet_centre = centre(wet_mask)
    lateral_centre = centre(lateral)
    field_centre = centre(marine_state)
    lateral_mix = jnp.zeros_like(field_centre)
    for neighbour in (to_east, to_west, to_north, to_south):
        face_coef = 0.5 * (lateral_centre + neighbour(lateral)) * wet_centre * neighbour(wet_mask)
        lateral_mix = lateral_mix + face_coef * (neighbour(marine_state) - field_centre)
    u_centre = field_centre[2]
    v_centre = field_centre[3]
    advection = u_centre * (to_east(marine_state) - to_west(marine_state)) * 0.5 + v_centre * (to_north(marine_state) - to_south(marine_state)) * 0.5
    tendency = lateral_mix - advection
    planet_rows = planet[1:-1]
    tend_u = tendency[2] + planet_rows * v_centre - (to_east(pressure) - to_west(pressure)) * 0.5
    tend_v = tendency[3] - planet_rows * u_centre - (to_north(pressure) - to_south(pressure)) * 0.5
    tendency = jnp.stack([tendency[0], tendency[1], tend_u, tend_v])
    updated = wet_centre * (field_centre + dt_step * tendency)
    return updated.reshape(4 * layer_total, updated.shape[2], updated.shape[3])


def vertical_mix(marine_state, wet_mask, ambient_diffusion):
    layer_total = marine_state.shape[1]
    density_now = density(marine_state[0], marine_state[1])
    stratification = density_now[1:] - density_now[:-1]
    coupling = ambient_diffusion[None] * (0.2 + 1.0 / (1.0 + 10.0 * jnp.maximum(stratification, 0.0))) * wet_mask[1:]
    zero_plane = jnp.zeros_like(ambient_diffusion)
    ratio_prev = zero_plane
    value_prev = jnp.zeros_like(marine_state[:, 0])
    ratio_list = []
    value_list = []
    for level in range(layer_total):
        lower_coef = coupling[level - 1] if level > 0 else zero_plane
        upper_coef = coupling[level] if level < layer_total - 1 else zero_plane
        pivot_value = 1.0 + lower_coef + upper_coef + lower_coef * ratio_prev
        ratio_prev = -upper_coef / pivot_value
        value_prev = (marine_state[:, level] + lower_coef * value_prev) / pivot_value
        ratio_list.append(ratio_prev)
        value_list.append(value_prev)
    current = value_list[layer_total - 1]
    solved = [current]
    for level in range(layer_total - 2, -1, -1):
        current = value_list[level] - ratio_list[level] * current
        solved.append(current)
    return jnp.stack(solved[::-1], axis=1)


def extend(combined, fold_signs, margin):
    lon_wrap = jnp.concatenate([combined[:, -margin:], combined, combined[:, :margin]], axis=1)
    mirror = jnp.roll(combined[:, ::-1, :], -FOLD_OFFSET, axis=1)
    mirror_wrap = jnp.concatenate([mirror[:, -margin:], mirror, mirror[:, :margin]], axis=1)
    folded = mirror_wrap[:, :, ::-1][:, :, :margin] * fold_signs[:, None, None]
    south_zero = jnp.zeros_like(lon_wrap[:, :, :margin])
    return jnp.concatenate([south_zero, lon_wrap, folded], axis=2)


def reference(thermal_anomaly, saltiness_anomaly, zonal_flow, meridional_flow, flooded_layer_number, sideways_diffusion, ambient_diffusion):
    layer_total = thermal_anomaly.shape[0]
    statics = jnp.stack([flooded_layer_number.astype(jnp.float32), sideways_diffusion])
    marine_state = jnp.concatenate([thermal_anomaly, saltiness_anomaly, zonal_flow, meridional_flow], axis=0)
    fold_signs = jnp.concatenate([jnp.ones((2 * layer_total,), jnp.float32), -jnp.ones((2 * layer_total,), jnp.float32), jnp.ones((2,), jnp.float32)])
    planet = coriolis_rows(-1, MERIDIAN_POINTS + 2, MERIDIAN_POINTS)
    for substep in range(SUBSTEPS):
        padded = extend(jnp.concatenate([marine_state, statics], axis=0), fold_signs, 1)
        marine_state = advance(padded, planet)
    level_index = jnp.arange(layer_total, dtype=jnp.float32)[:, None, None]
    wet_mask = (level_index < flooded_layer_number.astype(jnp.float32)[None]).astype(jnp.float32)
    final = vertical_mix(marine_state.reshape(4, layer_total, ZONAL_POINTS, MERIDIAN_POINTS), wet_mask, ambient_diffusion)
    return final[0], final[1], final[2], final[3]
```

```python
import functools

import jax
import jax.numpy as jnp
from jax import lax
from jax.experimental import pallas as pl
from jax.experimental.pallas import tpu as pltpu
from jax.sharding import PartitionSpec as P

SUBSTEPS = 2
DT = 0.05

LANES = 128
ROWS = 8
FLOOD_ROW = 0
MIX_ROW = 1


def density(temp, salt):
    return temp * (0.03 * salt - 0.05 * temp - 0.2) + 0.8 * salt


def parity():
    return lax.rem(lax.axis_index("lon"), 2)


def pack_kernel(levels, temp, salt, zonal, merid, flood, mix, tile, edge, sems):
    odd = parity()
    copies = []
    for f, field in enumerate((temp, salt, zonal, merid)):
        for c in range(2):
            slot = odd if c == 0 else 1 - odd
            copy = pltpu.make_async_copy(
                field.at[:, c, :], tile.at[slot, f, pl.ds(0, levels), :], sems.at[2 * f + c]
            )
            copy.start()
            copies.append(copy)
    padded = tile.shape[2]
    for copy in copies:
        copy.wait()
    zero = jnp.zeros((padded - levels, LANES), jnp.float32)
    for f in range(4):
        for s in range(2):
            tile[s, f, pl.ds(levels, padded - levels), :] = zero
    for c in range(2):
        slot = odd if c == 0 else 1 - odd
        tile[slot, 0, pl.ds(levels + FLOOD_ROW, 1), :] = flood[pl.ds(c, 1), :].astype(jnp.float32)
        tile[slot, 0, pl.ds(levels + MIX_ROW, 1), :] = mix[pl.ds(c, 1), :]
    lane = lax.broadcasted_iota(jnp.int32, (ROWS, LANES), 1)
    for b in range(padded // ROWS):
        rows = pl.ds(ROWS * b, ROWS)
        total = jnp.zeros((ROWS, LANES), jnp.float32)
        for f in range(4):
            for s in range(2):
                block = tile[s, f, rows, :]
                low = 8 * f + 2 * s
                total = jnp.where((lane >> 1) == low // 2, pltpu.roll(block, low, 1), total)
                high = low + 4
                total = jnp.where((lane >> 1) == high // 2, pltpu.roll(block, high + 2, 1), total)
        edge[rows, :] = total


def pack(fields, flood, mix):
    levels = fields[0].shape[0]
    padded = (levels + 2 + ROWS - 1) // ROWS * ROWS
    return pl.pallas_call(
        functools.partial(pack_kernel, levels),
        out_shape=(
            jax.ShapeDtypeStruct((2, 4, padded, LANES), jnp.float32),
            jax.ShapeDtypeStruct((padded, LANES), jnp.float32),
        ),
        in_specs=[pl.BlockSpec(memory_space=pltpu.HBM)] * 4 + [pl.BlockSpec(memory_space=pltpu.VMEM)] * 2,
        out_specs=(pl.BlockSpec(memory_space=pltpu.VMEM),) * 2,
        scratch_shapes=[pltpu.SemaphoreType.DMA((8,))],
    )(*fields, flood, mix)


def step_kernel(
    levels,
    lat_count,
    own,
    side_a,
    side_b,
    south,
    south_a,
    south_b,
    north,
    north_a,
    north_b,
    fold_1,
    fold_2,
    ambient,
    temp_out,
    salt_out,
    zonal_out,
    merid_out,
    edges,
    statics,
    columns,
    couple,
    state,
    ratio,
    sems,
):
    odd = parity()
    lat = lax.axis_index("lat")
    padded = own.shape[2]
    blocks = padded // ROWS
    lane = lax.broadcasted_iota(jnp.int32, (ROWS, LANES), 1)
    row = lax.broadcasted_iota(jnp.int32, (ROWS, LANES), 0)
    first_lane = lane == 0
    last_lane = lane == LANES - 1
    slot_1_lane = (lane == 1) | (lane == 2)
    south_lane = (lane == 0) | (lane == 2)

    def put_south(b, f, values):
        rows = pl.ds(pl.multiple_of(ROWS * b, ROWS), ROWS)
        for e in range(3):
            edges[e, f, rows, :] = values[e]

    def put_north(b, f, values):
        rows = pl.ds(pl.multiple_of(ROWS * b, ROWS), ROWS)
        for e in range(3):
            edges[e, f, rows, :] = jnp.where(south_lane, edges[e, f, rows, :], values[e])

    def each_block(body):
        @pl.loop(0, blocks)
        def _(b):
            body(b, pl.ds(pl.multiple_of(ROWS * b, ROWS), ROWS))

    def shift(x, source, target):
        return pltpu.roll(x, (target - source) % LANES, 1)

    @pl.when(lat == 0)
    def _():
        def body(b, rows):
            for f in range(4):
                put_south(b, f, [jnp.zeros((ROWS, LANES), jnp.float32)] * 3)

        each_block(body)

    @pl.when(lat > 0)
    def _():
        def body(b, rows):
            mid, at_a, at_b = south[rows, :], south_a[rows, :], south_b[rows, :]
            for f in range(4):
                far = shift(at_b, 8 * f + 5, 0)
                far = jnp.where(slot_1_lane, shift(at_a, 8 * f + 5, 0), far)
                put_south(b, f, [shift(mid, 8 * f + 5, 0), shift(mid, 8 * f + 4, 0), far])

        each_block(body)

    @pl.when(lat < lat_count - 1)
    def _():
        def body(b, rows):
            mid, at_a, at_b = north[rows, :], north_a[rows, :], north_b[rows, :]
            for f in range(4):
                far = shift(at_b, 8 * f, 127)
                far = jnp.where(slot_1_lane, shift(at_a, 8 * f, 127), far)
                put_north(b, f, [shift(mid, 8 * f, 127), shift(mid, 8 * f + 1, 127), far])

        each_block(body)

    for top_odd in range(2):

        @pl.when((lat == lat_count - 1) & (odd == top_odd))
        def _(top_odd=top_odd):
            def body(b, rows):
                near, other = fold_1[rows, :], fold_2[rows, :]
                if top_odd:
                    near, other = other, near
                for f in range(4):
                    mine = 8 * f + 4 + 2 * (1 - top_odd)
                    beside = 8 * f + 4 + 2 * top_odd
                    values = []
                    for source in (mine + 1, mine, beside + 1):
                        values.append(
                            jnp.where(slot_1_lane, shift(other, source, 1), shift(near, source, 127))
                        )
                    if f >= 2:
                        values = [-v for v in values]
                    put_north(b, f, values)

            each_block(body)

    def swap(x):
        return jnp.where(slot_1_lane, pltpu.roll(x, 2, 1), pltpu.roll(x, LANES - 2, 1))

    def to_slot(x, slot):
        return x if slot == 0 else pltpu.roll(x, LANES - 2, 1)

    def northern(x, edge):
        return jnp.where(last_lane, edge, pltpu.roll(x, LANES - 1, 1))

    def southern(x, edge):
        return jnp.where(first_lane, edge, pltpu.roll(x, 1, 1))

    def ring(own_0, own_1):
        return jnp.where(slot_1_lane, pltpu.roll(own_1, 2, 1), own_0)

    def static_row(ref, index, which):
        line = ref[index + (pl.ds(levels + which, 1), slice(None))]
        return jnp.broadcast_to(line, (ROWS, LANES))

    sigma = jnp.where(odd == 0, 1.0, -1.0).astype(jnp.float32)
    sources = {
        "own0": (own, (0, 0)),
        "own1": (own, (1, 0)),
        "near0": (side_b, (0, 0)),
        "near1": (side_a, (1, 0)),
        "far0": (side_b, (1, 0)),
        "far1": (side_a, (0, 0)),
        "rim": (edges, (0, 0)),
        "rim2": (edges, (1, 0)),
        "corner": (edges, (2, 0)),
    }
    held = {name: [static_row(r, i, w) for w in (FLOOD_ROW, MIX_ROW)] for name, (r, i) in sources.items()}

    def neighbours(get, name):
        if name == "rim":
            centre = get("rim")
            beside = ring(get("own0"), get("own1"))
            beyond = get("rim2")
            north_cell = jnp.where(south_lane, beside, beyond)
            south_cell = jnp.where(south_lane, beyond, beside)
            return swap(centre), get("corner"), north_cell, south_cell
        slot = int(name[-1])
        centre = get(name)
        if name.startswith("own"):
            inner, outer, edge = get("own%d" % (1 - slot)), get("near%d" % slot), get("rim")
        else:
            inner, outer, edge = get("own%d" % slot), get("far%d" % slot), get("corner")
        edge = to_slot(edge, slot)
        return inner, outer, northern(centre, edge), southern(centre, edge)

    cell_sets = ("own0", "own1", "near0", "near1", "rim")
    for n, name in enumerate(cell_sets):
        flood_at = neighbours(lambda k: held[k][0], name)
        mix_at = neighbours(lambda k: held[k][1], name)
        statics[n, 0] = held[name][0]
        for m in range(4):
            statics[n, 1 + m] = jnp.minimum(held[name][0], flood_at[m])
            statics[n, 5 + m] = (0.5 * DT) * (held[name][1] + mix_at[m])

    total_rows = LANES * lat_count
    place = lat * LANES + lane
    rim_place = lat * LANES + jnp.where(south_lane, -1, LANES)

    def turning(index):
        index = jnp.where(index >= total_rows, 2 * total_rows - 1 - index, index)
        return DT * (0.2 + index.astype(jnp.float32) / total_rows)

    planet = {True: turning(rim_place), False: turning(place)}
    sigma_of = {
        "own0": sigma,
        "near0": sigma,
        "own1": -sigma,
        "near1": -sigma,
        "rim": jnp.where(slot_1_lane, -sigma, sigma),
    }

    def running(x, carry):
        for step in (1, 2, 4):
            x = x + jnp.where(row >= step, pltpu.roll(x, step, 0), 0.0)
        x = x + carry
        return x, jnp.broadcast_to(x[ROWS - 1 :, :], (ROWS, LANES))

    def advance(name, level, fields, pressure):
        n = cell_sets.index(name)
        wet = level < statics[n, 0]
        weights = [jnp.where(level < statics[n, 1 + m], statics[n, 5 + m], 0.0) for m in range(4)]
        keep = jnp.where(wet, 1.0, 0.0)
        centre = keep - ((weights[0] + weights[1]) + (weights[2] + weights[3]))
        half = jnp.where(wet, 0.5 * DT, 0.0)
        along = half * sigma_of[name]
        flow_u, flow_v = fields[2][name], fields[3][name]
        drift_u = along * flow_u
        drift_v = half * flow_v
        inner, outer, north_w, south_w = (
            weights[0] - drift_u,
            weights[1] + drift_u,
            weights[2] - drift_v,
            weights[3] + drift_v,
        )
        out = []
        for f in range(4):
            cells = neighbours(lambda k, f=f: fields[f][k], name)
            value = centre * fields[f][name]
            value = value + ((inner * cells[0] + outer * cells[1]) + (north_w * cells[2] + south_w * cells[3]))
            out.append(value)
        cells = neighbours(lambda k: pressure[k], name)
        turn = keep * planet[name == "rim"]
        out[2] = out[2] + (turn * flow_v - (0.5 * along) * (cells[0] - cells[1]))
        out[3] = out[3] - (turn * flow_u + (0.5 * half) * (cells[2] - cells[3]))
        return out

    all_sets = ("own0", "own1", "near0", "near1", "far0", "far1", "rim", "rim2", "corner")
    zero = jnp.zeros((ROWS, LANES), jnp.float32)
    ambient_row = [
        jnp.broadcast_to(jnp.where(odd == s, ambient[0:1, :], ambient[1:2, :]), (ROWS, LANES)) for s in range(2)
    ]

    def block_body(b, carry):
        carry_1, carry_2, carry_3 = carry
        rows = pl.ds(pl.multiple_of(ROWS * b, ROWS), ROWS)
        level = (row + ROWS * b).astype(jnp.float32)
        fields = [{k: sources[k][0][sources[k][1][0], f, rows, :] for k in all_sets} for f in range(4)]
        pressure = {}
        next_1 = []
        for k, c in zip(all_sets, carry_1):
            pressure[k], c = running(density(fields[0][k], fields[1][k]), c)
            next_1.append(c)
        updated = {name: advance(name, level, fields, pressure) for name in cell_sets}
        fields = [{name: updated[name][f] for name in cell_sets} for f in range(4)]
        pressure = {}
        next_2 = []
        for k, c in zip(cell_sets, carry_2):
            pressure[k], c = running(density(fields[0][k], fields[1][k]), c)
            next_2.append(c)
        next_3 = []
        for s in range(2):
            final = advance("own%d" % s, level, fields, pressure)
            place_s = odd if s == 0 else 1 - odd
            dense = density(final[0], final[1])
            above = jnp.where(row == 0, carry_3[s], pltpu.roll(dense, 1, 0))
            next_3.append(jnp.broadcast_to(dense[ROWS - 1 :, :], (ROWS, LANES)))
            gate = (level < statics[s, 0]) & (level > 0.0)
            lower = ambient_row[s] * (0.2 + 1.0 / (1.0 + 10.0 * jnp.maximum(dense - above, 0.0)))
            lower = jnp.where(gate, lower, 0.0)
            for f in range(4):
                columns[2 * f + place_s, rows, :] = final[f]
                couple[2 * f + place_s, rows, :] = lower
        return tuple(next_1), tuple(next_2), tuple(next_3)

    lax.fori_loop(
        0, blocks, block_body, ((zero,) * len(all_sets), (zero,) * len(cell_sets), (zero,) * 2)
    )

    gain = jnp.ones((ROWS, LANES), jnp.float32)
    value = zero
    lower = zero
    for k in range(levels):
        upper = couple[:, k + 1, :]
        inverse = 1.0 / (gain + upper)
        value = (columns[:, k, :] + lower * value) * inverse
        share = upper * inverse
        state[k] = value
        ratio[k] = share
        gain = 1.0 + share * gain
        lower = upper
    current = value
    for k in range(levels - 2, -1, -1):
        current = state[k] + ratio[k] * current
        state[k] = current
    copies = []
    for f, out in enumerate((temp_out, salt_out, zonal_out, merid_out)):
        copy = pltpu.make_async_copy(state.at[:, pl.ds(2 * f, 2), :], out, sems.at[f])
        copy.start()
        copies.append(copy)
    for copy in copies:
        copy.wait()


def pairs_a(count):
    return [(i, i ^ 1) for i in range(count)]


def pairs_b(count, wrap):
    found = []
    for i in range(1, count - 1):
        found.append((i, i + 1 if i % 2 else i - 1))
    if wrap:
        found += [(0, count - 1), (count - 1, 0)]
    return found


def shards(temp, salt, zonal, merid, flood, mix, ambient):
    levels = temp.shape[0]
    lon_count = lax.axis_size("lon")
    lat_count = lax.axis_size("lat")
    axes = ("lon", "lat")
    tile, edge = pack((temp, salt, zonal, merid), flood, mix)
    lon_a, lon_b = pairs_a(lon_count), pairs_b(lon_count, True)

    def joint(lon_pairs, lat_pairs):
        return [
            (i * lat_count + m, j * lat_count + n) for i, j in lon_pairs for m, n in lat_pairs
        ]

    same = [(i, i) for i in range(lon_count)]
    side_b = lax.ppermute(tile, "lon", lon_b)
    side_a = lax.ppermute(tile, "lon", lon_a)
    rounds = [pairs_a(lat_count)] + ([pairs_b(lat_count, False)] if lat_count > 2 else [])
    got = [[lax.ppermute(edge, axes, joint(lon, lats)) for lon in (same, lon_a, lon_b)] for lats in rounds]
    if len(got) == 1:
        north = south = got[0]
    else:
        flip = lax.rem(lax.axis_index("lat"), 2) == 0
        north = [jnp.where(flip, x, y) for x, y in zip(*got)]
        south = [jnp.where(flip, y, x) for x, y in zip(*got)]
    top = [(lat_count - 1, lat_count - 1)]
    folds = [
        lax.ppermute(edge, axes, joint([(i, (lon_count - 1 - n - i) % lon_count) for i in range(lon_count)], top))
        for n in range(2)
    ]
    padded = tile.shape[2]
    vmem = pl.BlockSpec(memory_space=pltpu.VMEM)
    result = jax.ShapeDtypeStruct(temp.shape, jnp.float32)
    return pl.pallas_call(
        functools.partial(step_kernel, levels, lat_count),
        out_shape=(result,) * 4,
        in_specs=[vmem] * 12,
        out_specs=(pl.BlockSpec(memory_space=pltpu.HBM),) * 4,
        scratch_shapes=[
            pltpu.VMEM((3, 4, padded, LANES), jnp.float32),
            pltpu.VMEM((5, 9, ROWS, LANES), jnp.float32),
            pltpu.VMEM((ROWS, padded, LANES), jnp.float32),
            pltpu.VMEM((ROWS, padded, LANES), jnp.float32),
            pltpu.VMEM((levels, ROWS, LANES), jnp.float32),
            pltpu.VMEM((levels, ROWS, LANES), jnp.float32),
            pltpu.SemaphoreType.DMA((4,)),
        ],
    )(tile, side_a, side_b, *south, *north, *folds, ambient)


def solution(mesh):
    cube = P(None, "lon", "lat")
    plane = P("lon", "lat")
    return jax.shard_map(
        shards,
        mesh=mesh,
        in_specs=(cube,) * 4 + (plane,) * 3,
        out_specs=(cube,) * 4,
        check_vma=False,
    )
```

```python
import functools

import jax
import jax.numpy as jnp
from jax import lax
from jax.experimental import pallas as pl
from jax.experimental.pallas import tpu as pltpu
from jax.sharding import PartitionSpec as P

SUBSTEPS = 2
DT = 0.05

LANES = 128
VMEM_LIMIT = 16 << 20
ROWS = 8
FLOOD_ROW = 0
MIX_ROW = 1


def density(temp, salt):
    return temp * (0.03 * salt - 0.05 * temp - 0.2) + 0.8 * salt


def parity():
    return lax.rem(lax.axis_index("lon"), 2)


def pack_kernel(levels, temp, salt, zonal, merid, flood, mix, tile, edge, flood_here, mix_here, sems):
    odd = parity()
    copies = [
        pltpu.make_async_copy(flood, flood_here, sems.at[8]),
        pltpu.make_async_copy(mix, mix_here, sems.at[9]),
    ]
    for copy in copies:
        copy.start()
    for f, field in enumerate((temp, salt, zonal, merid)):
        for c in range(2):
            slot = odd if c == 0 else 1 - odd
            copy = pltpu.make_async_copy(
                field.at[:, c, :], tile.at[slot, f, pl.ds(0, levels), :], sems.at[2 * f + c]
            )
            copy.start()
            copies.append(copy)
    padded = tile.shape[2]
    for copy in copies:
        copy.wait()
    zero = jnp.zeros((padded - levels, LANES), jnp.float32)
    for f in range(4):
        for s in range(2):
            tile[s, f, pl.ds(levels, padded - levels), :] = zero
    for c in range(2):
        slot = odd if c == 0 else 1 - odd
        tile[slot, 0, pl.ds(levels + FLOOD_ROW, 1), :] = flood_here[pl.ds(c, 1), :].astype(jnp.float32)
        tile[slot, 0, pl.ds(levels + MIX_ROW, 1), :] = mix_here[pl.ds(c, 1), :]
    lane = lax.broadcasted_iota(jnp.int32, (ROWS, LANES), 1)
    for b in range(padded // ROWS):
        rows = pl.ds(ROWS * b, ROWS)
        total = jnp.zeros((ROWS, LANES), jnp.float32)
        for f in range(4):
            for s in range(2):
                block = tile[s, f, rows, :]
                low = 8 * f + 2 * s
                total = jnp.where((lane >> 1) == low // 2, pltpu.roll(block, low, 1), total)
                high = low + 4
                total = jnp.where((lane >> 1) == high // 2, pltpu.roll(block, high + 2, 1), total)
        edge[rows, :] = total


def pack(fields, flood, mix):
    levels = fields[0].shape[0]
    padded = (levels + 2 + ROWS - 1) // ROWS * ROWS
    return pl.pallas_call(
        functools.partial(pack_kernel, levels),
        out_shape=(
            jax.ShapeDtypeStruct((2, 4, padded, LANES), jnp.float32),
            jax.ShapeDtypeStruct((padded, LANES), jnp.float32),
        ),
        in_specs=[pl.BlockSpec(memory_space=pltpu.HBM)] * 6,
        out_specs=(pl.BlockSpec(memory_space=pltpu.VMEM),) * 2,
        scratch_shapes=[
            pltpu.VMEM(flood.shape, flood.dtype),
            pltpu.VMEM(mix.shape, mix.dtype),
            pltpu.SemaphoreType.DMA((10,)),
        ],
        compiler_params=pltpu.CompilerParams(vmem_limit_bytes=VMEM_LIMIT),
    )(*[pltpu.with_memory_space_constraint(x, pltpu.HBM) for x in (*fields, flood, mix)])


def step_kernel(
    levels,
    lat_count,
    own,
    side_a,
    side_b,
    south,
    south_a,
    south_b,
    north,
    north_a,
    north_b,
    fold_1,
    fold_even,
    fold_odd,
    ambient,
    temp_out,
    salt_out,
    zonal_out,
    merid_out,
    edges,
    statics,
    columns,
    couple,
    state,
    ratio,
    sems,
):
    odd = parity()
    lat = lax.axis_index("lat")
    padded = own.shape[2]
    blocks = padded // ROWS
    lane = lax.broadcasted_iota(jnp.int32, (ROWS, LANES), 1)
    row = lax.broadcasted_iota(jnp.int32, (ROWS, LANES), 0)
    first_lane = lane == 0
    last_lane = lane == LANES - 1
    slot_1_lane = (lane == 1) | (lane == 2)
    south_lane = (lane == 0) | (lane == 2)

    def put_south(b, f, values):
        rows = pl.ds(pl.multiple_of(ROWS * b, ROWS), ROWS)
        for e in range(3):
            edges[e, f, rows, :] = values[e]

    def put_north(b, f, values):
        rows = pl.ds(pl.multiple_of(ROWS * b, ROWS), ROWS)
        for e in range(3):
            edges[e, f, rows, :] = jnp.where(south_lane, edges[e, f, rows, :], values[e])

    def each_block(body):
        @pl.loop(0, blocks)
        def _(b):
            body(b, pl.ds(pl.multiple_of(ROWS * b, ROWS), ROWS))

    def shift(x, source, target):
        return pltpu.roll(x, (target - source) % LANES, 1)

    @pl.when(lat == 0)
    def _():
        def body(b, rows):
            for f in range(4):
                put_south(b, f, [jnp.zeros((ROWS, LANES), jnp.float32)] * 3)

        each_block(body)

    @pl.when(lat > 0)
    def _():
        def body(b, rows):
            mid, at_a, at_b = south[rows, :], south_a[rows, :], south_b[rows, :]
            for f in range(4):
                far = shift(at_b, 8 * f + 5, 0)
                far = jnp.where(slot_1_lane, shift(at_a, 8 * f + 5, 0), far)
                put_south(b, f, [shift(mid, 8 * f + 5, 0), shift(mid, 8 * f + 4, 0), far])

        each_block(body)

    @pl.when(lat < lat_count - 1)
    def _():
        def body(b, rows):
            mid, at_a, at_b = north[rows, :], north_a[rows, :], north_b[rows, :]
            for f in range(4):
                far = shift(at_b, 8 * f, 127)
                far = jnp.where(slot_1_lane, shift(at_a, 8 * f, 127), far)
                put_north(b, f, [shift(mid, 8 * f, 127), shift(mid, 8 * f + 1, 127), far])

        each_block(body)

    for top_odd in range(2):

        @pl.when((lat == lat_count - 1) & (odd == top_odd))
        def _(top_odd=top_odd):
            def body(b, rows):
                near, other = fold_1[rows, :], fold_even[rows, :]
                if top_odd:
                    near, other = fold_odd[rows, :], near
                for f in range(4):
                    mine = 8 * f + 4 + 2 * (1 - top_odd)
                    beside = 8 * f + 4 + 2 * top_odd
                    values = []
                    for source in (mine + 1, mine, beside + 1):
                        values.append(
                            jnp.where(slot_1_lane, shift(other, source, 1), shift(near, source, 127))
                        )
                    if f >= 2:
                        values = [-v for v in values]
                    put_north(b, f, values)

            each_block(body)

    def swap(x):
        return jnp.where(slot_1_lane, pltpu.roll(x, 2, 1), pltpu.roll(x, LANES - 2, 1))

    def to_slot(x, slot):
        return x if slot == 0 else pltpu.roll(x, LANES - 2, 1)

    def northern(x, edge):
        return jnp.where(last_lane, edge, pltpu.roll(x, LANES - 1, 1))

    def southern(x, edge):
        return jnp.where(first_lane, edge, pltpu.roll(x, 1, 1))

    def ring(own_0, own_1):
        return jnp.where(slot_1_lane, pltpu.roll(own_1, 2, 1), own_0)

    def static_row(ref, index, which):
        line = ref[index + (pl.ds(levels + which, 1), slice(None))]
        return jnp.broadcast_to(line, (ROWS, LANES))

    sigma = jnp.where(odd == 0, 1.0, -1.0).astype(jnp.float32)
    sources = {
        "own0": (own, (0, 0)),
        "own1": (own, (1, 0)),
        "near0": (side_b, (0, 0)),
        "near1": (side_a, (1, 0)),
        "far0": (side_b, (1, 0)),
        "far1": (side_a, (0, 0)),
        "rim": (edges, (0, 0)),
        "rim2": (edges, (1, 0)),
        "corner": (edges, (2, 0)),
    }
    held = {name: [static_row(r, i, w) for w in (FLOOD_ROW, MIX_ROW)] for name, (r, i) in sources.items()}

    def neighbours(get, name):
        if name == "rim":
            centre = get("rim")
            beside = ring(get("own0"), get("own1"))
            beyond = get("rim2")
            north_cell = jnp.where(south_lane, beside, beyond)
            south_cell = jnp.where(south_lane, beyond, beside)
            return swap(centre), get("corner"), north_cell, south_cell
        slot = int(name[-1])
        centre = get(name)
        if name.startswith("own"):
            inner, outer, edge = get("own%d" % (1 - slot)), get("near%d" % slot), get("rim")
        else:
            inner, outer, edge = get("own%d" % slot), get("far%d" % slot), get("corner")
        edge = to_slot(edge, slot)
        return inner, outer, northern(centre, edge), southern(centre, edge)

    cell_sets = ("own0", "own1", "near0", "near1", "rim")
    for n, name in enumerate(cell_sets):
        flood_at = neighbours(lambda k: held[k][0], name)
        mix_at = neighbours(lambda k: held[k][1], name)
        statics[n, 0] = held[name][0]
        for m in range(4):
            statics[n, 1 + m] = jnp.minimum(held[name][0], flood_at[m])
            statics[n, 5 + m] = (0.5 * DT) * (held[name][1] + mix_at[m])

    total_rows = LANES * lat_count
    place = lat * LANES + lane
    rim_place = lat * LANES + jnp.where(south_lane, -1, LANES)

    def turning(index):
        index = jnp.where(index >= total_rows, 2 * total_rows - 1 - index, index)
        return DT * (0.2 + index.astype(jnp.float32) / total_rows)

    planet = {True: turning(rim_place), False: turning(place)}
    sigma_of = {
        "own0": sigma,
        "near0": sigma,
        "own1": -sigma,
        "near1": -sigma,
        "rim": jnp.where(slot_1_lane, -sigma, sigma),
    }

    def running(x, carry):
        for step in (1, 2, 4):
            x = x + jnp.where(row >= step, pltpu.roll(x, step, 0), 0.0)
        x = x + carry
        return x, jnp.broadcast_to(x[ROWS - 1 :, :], (ROWS, LANES))

    def advance(name, level, fields, pressure):
        n = cell_sets.index(name)
        wet = level < statics[n, 0]
        weights = [jnp.where(level < statics[n, 1 + m], statics[n, 5 + m], 0.0) for m in range(4)]
        keep = jnp.where(wet, 1.0, 0.0)
        centre = keep - ((weights[0] + weights[1]) + (weights[2] + weights[3]))
        half = jnp.where(wet, 0.5 * DT, 0.0)
        along = half * sigma_of[name]
        flow_u, flow_v = fields[2][name], fields[3][name]
        drift_u = along * flow_u
        drift_v = half * flow_v
        inner, outer, north_w, south_w = (
            weights[0] - drift_u,
            weights[1] + drift_u,
            weights[2] - drift_v,
            weights[3] + drift_v,
        )
        out = []
        for f in range(4):
            cells = neighbours(lambda k, f=f: fields[f][k], name)
            value = centre * fields[f][name]
            value = value + ((inner * cells[0] + outer * cells[1]) + (north_w * cells[2] + south_w * cells[3]))
            out.append(value)
        cells = neighbours(lambda k: pressure[k], name)
        turn = keep * planet[name == "rim"]
        out[2] = out[2] + (turn * flow_v - (0.5 * along) * (cells[0] - cells[1]))
        out[3] = out[3] - (turn * flow_u + (0.5 * half) * (cells[2] - cells[3]))
        return out

    all_sets = ("own0", "own1", "near0", "near1", "far0", "far1", "rim", "rim2", "corner")
    zero = jnp.zeros((ROWS, LANES), jnp.float32)
    ambient_row = [
        jnp.broadcast_to(jnp.where(odd == s, ambient[0:1, :], ambient[1:2, :]), (ROWS, LANES)) for s in range(2)
    ]

    def block_body(b, carry):
        carry_1, carry_2, carry_3 = carry
        rows = pl.ds(pl.multiple_of(ROWS * b, ROWS), ROWS)
        level = (row + ROWS * b).astype(jnp.float32)
        fields = [{k: sources[k][0][sources[k][1][0], f, rows, :] for k in all_sets} for f in range(4)]
        pressure = {}
        next_1 = []
        for k, c in zip(all_sets, carry_1):
            pressure[k], c = running(density(fields[0][k], fields[1][k]), c)
            next_1.append(c)
        updated = {name: advance(name, level, fields, pressure) for name in cell_sets}
        fields = [{name: updated[name][f] for name in cell_sets} for f in range(4)]
        pressure = {}
        next_2 = []
        for k, c in zip(cell_sets, carry_2):
            pressure[k], c = running(density(fields[0][k], fields[1][k]), c)
            next_2.append(c)
        next_3 = []
        for s in range(2):
            final = advance("own%d" % s, level, fields, pressure)
            place_s = odd if s == 0 else 1 - odd
            dense = density(final[0], final[1])
            above = jnp.where(row == 0, carry_3[s], pltpu.roll(dense, 1, 0))
            next_3.append(jnp.broadcast_to(dense[ROWS - 1 :, :], (ROWS, LANES)))
            gate = (level < statics[s, 0]) & (level > 0.0)
            lower = ambient_row[s] * (0.2 + 1.0 / (1.0 + 10.0 * jnp.maximum(dense - above, 0.0)))
            lower = jnp.where(gate, lower, 0.0)
            for f in range(4):
                columns[2 * f + place_s, rows, :] = final[f]
                couple[2 * f + place_s, rows, :] = lower
        return tuple(next_1), tuple(next_2), tuple(next_3)

    lax.fori_loop(
        0, blocks, block_body, ((zero,) * len(all_sets), (zero,) * len(cell_sets), (zero,) * 2)
    )

    gain = jnp.ones((ROWS, LANES), jnp.float32)
    value = zero
    lower = zero
    for k in range(levels):
        upper = couple[:, k + 1, :]
        inverse = 1.0 / (gain + upper)
        value = (columns[:, k, :] + lower * value) * inverse
        share = upper * inverse
        state[k] = value
        ratio[k] = share
        gain = 1.0 + share * gain
        lower = upper
    current = value
    for k in range(levels - 2, -1, -1):
        current = state[k] + ratio[k] * current
        state[k] = current
    copies = []
    for f, out in enumerate((temp_out, salt_out, zonal_out, merid_out)):
        copy = pltpu.make_async_copy(state.at[:, pl.ds(2 * f, 2), :], out, sems.at[f])
        copy.start()
        copies.append(copy)
    for copy in copies:
        copy.wait()


def pairs_a(count):
    return [(i, i ^ 1) for i in range(count)]


def pairs_b(count, wrap):
    found = []
    for i in range(1, count - 1):
        found.append((i, i + 1 if i % 2 else i - 1))
    if wrap:
        found += [(0, count - 1), (count - 1, 0)]
    return found


def shards(temp, salt, zonal, merid, flood, mix, ambient):
    levels = temp.shape[0]
    lon_count = lax.axis_size("lon")
    lat_count = lax.axis_size("lat")
    axes = ("lon", "lat")
    tile, edge = pack((temp, salt, zonal, merid), flood, mix)
    lon_a, lon_b = pairs_a(lon_count), pairs_b(lon_count, True)

    def joint(lon_pairs, lat_pairs):
        return [
            (i * lat_count + m, j * lat_count + n) for i, j in lon_pairs for m, n in lat_pairs
        ]

    same = [(i, i) for i in range(lon_count)]
    side_b = lax.ppermute(tile, "lon", lon_b)
    side_a = lax.ppermute(tile, "lon", lon_a)
    top = [(lat_count - 1, lat_count - 1)]
    mirror = [(i, lon_count - 1 - i) for i in range(lon_count)]
    mirror_odd = [(i, (lon_count - 2 - i) % lon_count) for i in range(1, lon_count, 2)]
    fold_1 = lax.ppermute(edge, axes, joint(mirror, top))
    fold_2 = lax.ppermute(edge, axes, joint(mirror_odd, top))
    rounds = [pairs_a(lat_count)] + ([pairs_b(lat_count, False)] if lat_count > 2 else [])
    got = []
    for lats in rounds:
        at_b, mid = [lax.ppermute(edge, axes, joint(lon, lats)) for lon in (lon_b, same)]
        got.append([mid, lax.ppermute(mid, "lon", lon_a), at_b])
    if len(got) == 1:
        north = south = got[0]
    else:
        flip = lax.rem(lax.axis_index("lat"), 2) == 0
        north = [jnp.where(flip, x, y) for x, y in zip(*got)]
        south = [jnp.where(flip, y, x) for x, y in zip(*got)]
    folds = [fold_1, lax.ppermute(fold_1, "lon", lon_a), fold_2]
    padded = tile.shape[2]
    vmem = pl.BlockSpec(memory_space=pltpu.VMEM)
    result = jax.ShapeDtypeStruct(temp.shape, jnp.float32)
    return pl.pallas_call(
        functools.partial(step_kernel, levels, lat_count),
        out_shape=(result,) * 4,
        in_specs=[vmem] * 13,
        out_specs=(pl.BlockSpec(memory_space=pltpu.HBM),) * 4,
        scratch_shapes=[
            pltpu.VMEM((3, 4, padded, LANES), jnp.float32),
            pltpu.VMEM((5, 9, ROWS, LANES), jnp.float32),
            pltpu.VMEM((ROWS, padded, LANES), jnp.float32),
            pltpu.VMEM((ROWS, padded, LANES), jnp.float32),
            pltpu.VMEM((levels, ROWS, LANES), jnp.float32),
            pltpu.VMEM((levels, ROWS, LANES), jnp.float32),
            pltpu.SemaphoreType.DMA((4,)),
        ],
        compiler_params=pltpu.CompilerParams(vmem_limit_bytes=VMEM_LIMIT),
    )(tile, side_a, side_b, *south, *north, *folds, ambient)


def solution(mesh):
    cube = P(None, "lon", "lat")
    plane = P("lon", "lat")
    return jax.shard_map(
        shards,
        mesh=mesh,
        in_specs=(cube,) * 4 + (plane,) * 3,
        out_specs=(cube,) * 4,
        check_vma=False,
    )
```

```python
import functools

import jax
import jax.numpy as jnp
from jax import lax
from jax.experimental import pallas as pl
from jax.experimental.pallas import tpu as pltpu
from jax.sharding import PartitionSpec as P

SUBSTEPS = 2
DT = 0.05

LANES = 128
VMEM_LIMIT = 16 << 20
RESCALE = 16
ROWS = 8
FLOOD_ROW = 0
MIX_ROW = 1


def density(temp, salt):
    return temp * (0.03 * salt - 0.05 * temp - 0.2) + 0.8 * salt


def parity():
    return lax.rem(lax.axis_index("lon"), 2)


def pack_kernel(levels, temp, salt, zonal, merid, flood, mix, tile, edge, flood_here, mix_here, sems):
    odd = parity()
    copies = [
        pltpu.make_async_copy(flood, flood_here, sems.at[8]),
        pltpu.make_async_copy(mix, mix_here, sems.at[9]),
    ]
    for copy in copies:
        copy.start()
    for f, field in enumerate((temp, salt, zonal, merid)):
        for c in range(2):
            slot = odd if c == 0 else 1 - odd
            copy = pltpu.make_async_copy(
                field.at[:, c, :], tile.at[slot, f, pl.ds(0, levels), :], sems.at[2 * f + c]
            )
            copy.start()
            copies.append(copy)
    padded = tile.shape[2]
    for copy in copies:
        copy.wait()
    zero = jnp.zeros((padded - levels, LANES), jnp.float32)
    for f in range(4):
        for s in range(2):
            tile[s, f, pl.ds(levels, padded - levels), :] = zero
    for c in range(2):
        slot = odd if c == 0 else 1 - odd
        tile[slot, 0, pl.ds(levels + FLOOD_ROW, 1), :] = flood_here[pl.ds(c, 1), :].astype(jnp.float32)
        tile[slot, 0, pl.ds(levels + MIX_ROW, 1), :] = mix_here[pl.ds(c, 1), :]
    lane = lax.broadcasted_iota(jnp.int32, (ROWS, LANES), 1)
    for b in range(padded // ROWS):
        rows = pl.ds(ROWS * b, ROWS)
        total = jnp.zeros((ROWS, LANES), jnp.float32)
        for f in range(4):
            for s in range(2):
                block = tile[s, f, rows, :]
                low = 8 * f + 2 * s
                total = jnp.where((lane >> 1) == low // 2, pltpu.roll(block, low, 1), total)
                high = low + 4
                total = jnp.where((lane >> 1) == high // 2, pltpu.roll(block, high + 2, 1), total)
        edge[rows, :] = total


def pack(fields, flood, mix):
    levels = fields[0].shape[0]
    padded = (levels + 2 + ROWS - 1) // ROWS * ROWS
    return pl.pallas_call(
        functools.partial(pack_kernel, levels),
        out_shape=(
            jax.ShapeDtypeStruct((2, 4, padded, LANES), jnp.float32),
            jax.ShapeDtypeStruct((padded, LANES), jnp.float32),
        ),
        in_specs=[pl.BlockSpec(memory_space=pltpu.HBM)] * 6,
        out_specs=(pl.BlockSpec(memory_space=pltpu.VMEM),) * 2,
        scratch_shapes=[
            pltpu.VMEM(flood.shape, flood.dtype),
            pltpu.VMEM(mix.shape, mix.dtype),
            pltpu.SemaphoreType.DMA((10,)),
        ],
        compiler_params=pltpu.CompilerParams(vmem_limit_bytes=VMEM_LIMIT),
    )(*[pltpu.with_memory_space_constraint(x, pltpu.HBM) for x in (*fields, flood, mix)])


def step_kernel(
    levels,
    lat_count,
    own,
    side_a,
    side_b,
    south,
    south_a,
    south_b,
    north,
    north_a,
    north_b,
    fold_1,
    fold_even,
    fold_odd,
    ambient,
    temp_out,
    salt_out,
    zonal_out,
    merid_out,
    edges,
    statics,
    columns,
    couple,
    state,
    ratio,
    sems,
):
    odd = parity()
    lat = lax.axis_index("lat")
    padded = own.shape[2]
    blocks = padded // ROWS
    lane = lax.broadcasted_iota(jnp.int32, (ROWS, LANES), 1)
    row = lax.broadcasted_iota(jnp.int32, (ROWS, LANES), 0)
    first_lane = lane == 0
    last_lane = lane == LANES - 1
    slot_1_lane = (lane == 1) | (lane == 2)
    south_lane = (lane == 0) | (lane == 2)

    def put_south(b, f, values):
        rows = pl.ds(ROWS * b, ROWS)
        for e in range(3):
            edges[e, f, rows, :] = values[e]

    def put_north(b, f, values):
        rows = pl.ds(ROWS * b, ROWS)
        for e in range(3):
            edges[e, f, rows, :] = jnp.where(south_lane, edges[e, f, rows, :], values[e])

    def each_block(body):
        for b in range(blocks):
            body(b, pl.ds(ROWS * b, ROWS))

    def shift(x, source, target):
        return pltpu.roll(x, (target - source) % LANES, 1)

    @pl.when(lat == 0)
    def _():
        def body(b, rows):
            for f in range(4):
                put_south(b, f, [jnp.zeros((ROWS, LANES), jnp.float32)] * 3)

        each_block(body)

    @pl.when(lat > 0)
    def _():
        def body(b, rows):
            mid, at_a, at_b = south[rows, :], south_a[rows, :], south_b[rows, :]
            for f in range(4):
                far = shift(at_b, 8 * f + 5, 0)
                far = jnp.where(slot_1_lane, shift(at_a, 8 * f + 5, 0), far)
                put_south(b, f, [shift(mid, 8 * f + 5, 0), shift(mid, 8 * f + 4, 0), far])

        each_block(body)

    @pl.when(lat < lat_count - 1)
    def _():
        def body(b, rows):
            mid, at_a, at_b = north[rows, :], north_a[rows, :], north_b[rows, :]
            for f in range(4):
                far = shift(at_b, 8 * f, 127)
                far = jnp.where(slot_1_lane, shift(at_a, 8 * f, 127), far)
                put_north(b, f, [shift(mid, 8 * f, 127), shift(mid, 8 * f + 1, 127), far])

        each_block(body)

    for top_odd in range(2):

        @pl.when((lat == lat_count - 1) & (odd == top_odd))
        def _(top_odd=top_odd):
            def body(b, rows):
                near, other = fold_1[rows, :], fold_even[rows, :]
                if top_odd:
                    near, other = fold_odd[rows, :], near
                for f in range(4):
                    mine = 8 * f + 4 + 2 * (1 - top_odd)
                    beside = 8 * f + 4 + 2 * top_odd
                    values = []
                    for source in (mine + 1, mine, beside + 1):
                        values.append(
                            jnp.where(slot_1_lane, shift(other, source, 1), shift(near, source, 127))
                        )
                    if f >= 2:
                        values = [-v for v in values]
                    put_north(b, f, values)

            each_block(body)

    def swap(x):
        return jnp.where(slot_1_lane, pltpu.roll(x, 2, 1), pltpu.roll(x, LANES - 2, 1))

    def to_slot(x, slot):
        return x if slot == 0 else pltpu.roll(x, LANES - 2, 1)

    def northern(x, edge):
        return jnp.where(last_lane, edge, pltpu.roll(x, LANES - 1, 1))

    def southern(x, edge):
        return jnp.where(first_lane, edge, pltpu.roll(x, 1, 1))

    def ring(own_0, own_1):
        return jnp.where(slot_1_lane, pltpu.roll(own_1, 2, 1), own_0)

    def static_row(ref, index, which):
        line = ref[index + (pl.ds(levels + which, 1), slice(None))]
        return jnp.broadcast_to(line, (ROWS, LANES))

    sigma = jnp.where(odd == 0, 1.0, -1.0).astype(jnp.float32)
    sources = {
        "own0": (own, (0, 0)),
        "own1": (own, (1, 0)),
        "near0": (side_b, (0, 0)),
        "near1": (side_a, (1, 0)),
        "far0": (side_b, (1, 0)),
        "far1": (side_a, (0, 0)),
        "rim": (edges, (0, 0)),
        "rim2": (edges, (1, 0)),
        "corner": (edges, (2, 0)),
    }
    held = {name: [static_row(r, i, w) for w in (FLOOD_ROW, MIX_ROW)] for name, (r, i) in sources.items()}

    def neighbours(get, name):
        if name == "rim":
            centre = get("rim")
            beside = ring(get("own0"), get("own1"))
            beyond = get("rim2")
            north_cell = jnp.where(south_lane, beside, beyond)
            south_cell = jnp.where(south_lane, beyond, beside)
            return swap(centre), get("corner"), north_cell, south_cell
        slot = int(name[-1])
        centre = get(name)
        if name.startswith("own"):
            inner, outer, edge = get("own%d" % (1 - slot)), get("near%d" % slot), get("rim")
        else:
            inner, outer, edge = get("own%d" % slot), get("far%d" % slot), get("corner")
        edge = to_slot(edge, slot)
        return inner, outer, northern(centre, edge), southern(centre, edge)

    cell_sets = ("own0", "own1", "near0", "near1", "rim")
    for n, name in enumerate(cell_sets):
        flood_at = neighbours(lambda k: held[k][0], name)
        mix_at = neighbours(lambda k: held[k][1], name)
        statics[n, 0] = held[name][0]
        for m in range(4):
            statics[n, 1 + m] = jnp.minimum(held[name][0], flood_at[m])
            statics[n, 5 + m] = (0.5 * DT) * (held[name][1] + mix_at[m])

    total_rows = LANES * lat_count
    place = lat * LANES + lane
    rim_place = lat * LANES + jnp.where(south_lane, -1, LANES)

    def turning(index):
        index = jnp.where(index >= total_rows, 2 * total_rows - 1 - index, index)
        return DT * (0.2 + index.astype(jnp.float32) / total_rows)

    planet = {True: turning(rim_place), False: turning(place)}
    sigma_of = {
        "own0": sigma,
        "near0": sigma,
        "own1": -sigma,
        "near1": -sigma,
        "rim": jnp.where(slot_1_lane, -sigma, sigma),
    }

    def running(x, carry):
        for step in (1, 2, 4):
            x = x + jnp.where(row >= step, pltpu.roll(x, step, 0), 0.0)
        x = x + carry
        return x, jnp.broadcast_to(x[ROWS - 1 :, :], (ROWS, LANES))

    def advance(name, level, fields, pressure):
        n = cell_sets.index(name)
        wet = level < statics[n, 0]
        weights = [jnp.where(level < statics[n, 1 + m], statics[n, 5 + m], 0.0) for m in range(4)]
        keep = jnp.where(wet, 1.0, 0.0)
        centre = keep - ((weights[0] + weights[1]) + (weights[2] + weights[3]))
        half = jnp.where(wet, 0.5 * DT, 0.0)
        along = half * sigma_of[name]
        flow_u, flow_v = fields[2][name], fields[3][name]
        drift_u = along * flow_u
        drift_v = half * flow_v
        inner, outer, north_w, south_w = (
            weights[0] - drift_u,
            weights[1] + drift_u,
            weights[2] - drift_v,
            weights[3] + drift_v,
        )
        out = []
        for f in range(4):
            cells = neighbours(lambda k, f=f: fields[f][k], name)
            value = centre * fields[f][name]
            value = value + ((inner * cells[0] + outer * cells[1]) + (north_w * cells[2] + south_w * cells[3]))
            out.append(value)
        cells = neighbours(lambda k: pressure[k], name)
        turn = keep * planet[name == "rim"]
        out[2] = out[2] + (turn * flow_v - (0.5 * along) * (cells[0] - cells[1]))
        out[3] = out[3] - (turn * flow_u + (0.5 * half) * (cells[2] - cells[3]))
        return out

    all_sets = ("own0", "own1", "near0", "near1", "far0", "far1", "rim", "rim2", "corner")
    zero = jnp.zeros((ROWS, LANES), jnp.float32)
    ambient_row = [
        jnp.broadcast_to(jnp.where(odd == s, ambient[0:1, :], ambient[1:2, :]), (ROWS, LANES)) for s in range(2)
    ]

    def block_body(b, carry):
        carry_1, carry_2, carry_3 = carry
        rows = pl.ds(pl.multiple_of(ROWS * b, ROWS), ROWS)
        level = (row + ROWS * b).astype(jnp.float32)
        fields = [{k: sources[k][0][sources[k][1][0], f, rows, :] for k in all_sets} for f in range(4)]
        pressure = {}
        next_1 = []
        for k, c in zip(all_sets, carry_1):
            pressure[k], c = running(density(fields[0][k], fields[1][k]), c)
            next_1.append(c)
        updated = {name: advance(name, level, fields, pressure) for name in cell_sets}
        fields = [{name: updated[name][f] for name in cell_sets} for f in range(4)]
        pressure = {}
        next_2 = []
        for k, c in zip(cell_sets, carry_2):
            pressure[k], c = running(density(fields[0][k], fields[1][k]), c)
            next_2.append(c)
        next_3 = []
        for s in range(2):
            final = advance("own%d" % s, level, fields, pressure)
            place_s = odd if s == 0 else 1 - odd
            dense = density(final[0], final[1])
            above = jnp.where(row == 0, carry_3[s], pltpu.roll(dense, 1, 0))
            next_3.append(jnp.broadcast_to(dense[ROWS - 1 :, :], (ROWS, LANES)))
            gate = (level < statics[s, 0]) & (level > 0.0)
            lower = ambient_row[s] * (0.2 + 1.0 / (1.0 + 10.0 * jnp.maximum(dense - above, 0.0)))
            lower = jnp.where(gate, lower, 0.0)
            for f in range(4):
                columns[rows, 2 * f + place_s, :] = final[f]
                couple[rows, 2 * f + place_s, :] = lower
        return tuple(next_1), tuple(next_2), tuple(next_3)

    lax.fori_loop(
        0, blocks, block_body, ((zero,) * len(all_sets), (zero,) * len(cell_sets), (zero,) * 2), unroll=blocks
    )

    top = jnp.ones((ROWS, LANES), jnp.float32)
    bottom = top
    value = zero
    lower = zero
    for k in range(levels):
        upper = couple[k + 1]
        grown = top + upper * bottom
        inverse = bottom / grown
        value = columns[k] * inverse + (lower * inverse) * value
        state[k] = value
        ratio[k] = upper * inverse
        top = grown + upper * top
        bottom = grown
        if k % RESCALE == RESCALE - 1:
            scale = 1.0 / bottom
            top, bottom = top * scale, jnp.ones_like(bottom)
        lower = upper
    current = value
    for k in range(levels - 2, -1, -1):
        current = state[k] + ratio[k] * current
        state[k] = current
    copies = []
    for f, out in enumerate((temp_out, salt_out, zonal_out, merid_out)):
        copy = pltpu.make_async_copy(state.at[:, pl.ds(2 * f, 2), :], out, sems.at[f])
        copy.start()
        copies.append(copy)
    for copy in copies:
        copy.wait()


def pairs_a(count):
    return [(i, i ^ 1) for i in range(count)]


def pairs_b(count, wrap):
    found = []
    for i in range(1, count - 1):
        found.append((i, i + 1 if i % 2 else i - 1))
    if wrap:
        found += [(0, count - 1), (count - 1, 0)]
    return found


def shards(temp, salt, zonal, merid, flood, mix, ambient):
    levels = temp.shape[0]
    lon_count = lax.axis_size("lon")
    lat_count = lax.axis_size("lat")
    axes = ("lon", "lat")
    tile, edge = pack((temp, salt, zonal, merid), flood, mix)
    lon_a, lon_b = pairs_a(lon_count), pairs_b(lon_count, True)

    def joint(lon_pairs, lat_pairs):
        return [
            (i * lat_count + m, j * lat_count + n) for i, j in lon_pairs for m, n in lat_pairs
        ]

    same = [(i, i) for i in range(lon_count)]
    side_b = lax.ppermute(tile, "lon", lon_b)
    side_a = lax.ppermute(tile, "lon", lon_a)
    top = [(lat_count - 1, lat_count - 1)]
    mirror = [(i, lon_count - 1 - i) for i in range(lon_count)]
    mirror_odd = [(i, (lon_count - 2 - i) % lon_count) for i in range(1, lon_count, 2)]
    fold_1 = lax.ppermute(edge, axes, joint(mirror, top))
    fold_2 = lax.ppermute(edge, axes, joint(mirror_odd, top))
    rounds = [pairs_a(lat_count)] + ([pairs_b(lat_count, False)] if lat_count > 2 else [])
    got = []
    for lats in rounds:
        at_b, mid = [lax.ppermute(edge, axes, joint(lon, lats)) for lon in (lon_b, same)]
        got.append([mid, lax.ppermute(mid, "lon", lon_a), at_b])
    if len(got) == 1:
        north = south = got[0]
    else:
        flip = lax.rem(lax.axis_index("lat"), 2) == 0
        north = [jnp.where(flip, x, y) for x, y in zip(*got)]
        south = [jnp.where(flip, y, x) for x, y in zip(*got)]
    folds = [fold_1, lax.ppermute(fold_1, "lon", lon_a), fold_2]
    padded = tile.shape[2]
    vmem = pl.BlockSpec(memory_space=pltpu.VMEM)
    result = jax.ShapeDtypeStruct(temp.shape, jnp.float32)
    return pl.pallas_call(
        functools.partial(step_kernel, levels, lat_count),
        out_shape=(result,) * 4,
        in_specs=[vmem] * 13,
        out_specs=(pl.BlockSpec(memory_space=pltpu.HBM),) * 4,
        scratch_shapes=[
            pltpu.VMEM((3, 4, padded, LANES), jnp.float32),
            pltpu.VMEM((5, 9, ROWS, LANES), jnp.float32),
            pltpu.VMEM((padded, ROWS, LANES), jnp.float32),
            pltpu.VMEM((padded, ROWS, LANES), jnp.float32),
            pltpu.VMEM((levels, ROWS, LANES), jnp.float32),
            pltpu.VMEM((levels, ROWS, LANES), jnp.float32),
            pltpu.SemaphoreType.DMA((4,)),
        ],
        compiler_params=pltpu.CompilerParams(vmem_limit_bytes=VMEM_LIMIT),
    )(tile, side_a, side_b, *south, *north, *folds, ambient)


def solution(mesh):
    cube = P(None, "lon", "lat")
    plane = P("lon", "lat")
    return jax.shard_map(
        shards,
        mesh=mesh,
        in_specs=(cube,) * 4 + (plane,) * 3,
        out_specs=(cube,) * 4,
        check_vma=False,
    )
```

```python
import functools

import jax
import jax.numpy as jnp
from jax import lax
from jax.experimental import pallas as pl
from jax.experimental.pallas import tpu as pltpu
from jax.sharding import PartitionSpec as P

SUBSTEPS = 2
DT = 0.05

LANES = 128
VMEM_LIMIT = 16 << 20
RESCALE = 16
ROWS = 8
FLOOD_ROW = 0
MIX_ROW = 1


def density(temp, salt):
    return temp * (0.03 * salt - 0.05 * temp - 0.2) + 0.8 * salt


def parity():
    return lax.rem(lax.axis_index("lon"), 2)


def pack_kernel(levels, temp, salt, zonal, merid, flood, mix, tile, edge, flood_here, mix_here, sems):
    odd = parity()
    copies = [
        pltpu.make_async_copy(flood, flood_here, sems.at[8]),
        pltpu.make_async_copy(mix, mix_here, sems.at[9]),
    ]
    for copy in copies:
        copy.start()
    for f, field in enumerate((temp, salt, zonal, merid)):
        for c in range(2):
            slot = odd if c == 0 else 1 - odd
            copy = pltpu.make_async_copy(
                field.at[:, c, :], tile.at[slot, f, pl.ds(0, levels), :], sems.at[2 * f + c]
            )
            copy.start()
            copies.append(copy)
    padded = tile.shape[2]
    for copy in copies:
        copy.wait()
    zero = jnp.zeros((padded - levels, LANES), jnp.float32)
    for f in range(4):
        for s in range(2):
            tile[s, f, pl.ds(levels, padded - levels), :] = zero
    for c in range(2):
        slot = odd if c == 0 else 1 - odd
        tile[slot, 0, pl.ds(levels + FLOOD_ROW, 1), :] = flood_here[pl.ds(c, 1), :].astype(jnp.float32)
        tile[slot, 0, pl.ds(levels + MIX_ROW, 1), :] = mix_here[pl.ds(c, 1), :]
    lane = lax.broadcasted_iota(jnp.int32, (ROWS, LANES), 1)
    for b in range(padded // ROWS):
        rows = pl.ds(ROWS * b, ROWS)
        total = jnp.zeros((ROWS, LANES), jnp.float32)
        for f in range(4):
            for s in range(2):
                block = tile[s, f, rows, :]
                low = 8 * f + 2 * s
                total = jnp.where((lane >> 1) == low // 2, pltpu.roll(block, low, 1), total)
                high = low + 4
                total = jnp.where((lane >> 1) == high // 2, pltpu.roll(block, high + 2, 1), total)
        edge[rows, :] = total


def pack(fields, flood, mix):
    levels = fields[0].shape[0]
    padded = (levels + 2 + ROWS - 1) // ROWS * ROWS
    return pl.pallas_call(
        functools.partial(pack_kernel, levels),
        out_shape=(
            jax.ShapeDtypeStruct((2, 4, padded, LANES), jnp.float32),
            jax.ShapeDtypeStruct((padded, LANES), jnp.float32),
        ),
        in_specs=[pl.BlockSpec(memory_space=pltpu.HBM)] * 6,
        out_specs=(pl.BlockSpec(memory_space=pltpu.VMEM),) * 2,
        scratch_shapes=[
            pltpu.VMEM(flood.shape, flood.dtype),
            pltpu.VMEM(mix.shape, mix.dtype),
            pltpu.SemaphoreType.DMA((10,)),
        ],
        compiler_params=pltpu.CompilerParams(vmem_limit_bytes=VMEM_LIMIT),
    )(*[pltpu.with_memory_space_constraint(x, pltpu.HBM) for x in (*fields, flood, mix)])


def edge_kernel(lat_count, *refs):
    readers = [lambda rows, ref=ref: ref[rows, :] for ref in refs[:-1]]
    south = [readers[i] for i in (5, 7, 3)]
    north = [readers[i] for i in (6, 8, 4)]
    folds = [readers[i] for i in (1, 2, 0)]
    fill_edges(lat_count, south, north, folds, refs[-1])


def fill_edges(lat_count, south, north, folds, edges):
    odd = parity()
    lat = lax.axis_index("lat")
    blocks = edges.shape[2] // ROWS
    lane = lax.broadcasted_iota(jnp.int32, (ROWS, LANES), 1)
    slot_1_lane = (lane == 1) | (lane == 2)
    south_lane = (lane == 0) | (lane == 2)

    def put_south(b, f, values):
        rows = pl.ds(ROWS * b, ROWS)
        for e in range(3):
            edges[e, f, rows, :] = values[e]

    def put_north(b, f, values):
        rows = pl.ds(ROWS * b, ROWS)
        for e in range(3):
            edges[e, f, rows, :] = jnp.where(south_lane, edges[e, f, rows, :], values[e])

    def each_block(body):
        for b in range(blocks):
            body(b, pl.ds(ROWS * b, ROWS))

    def shift(x, source, target):
        return pltpu.roll(x, (target - source) % LANES, 1)

    @pl.when(lat == 0)
    def _():
        def body(b, rows):
            for f in range(4):
                put_south(b, f, [jnp.zeros((ROWS, LANES), jnp.float32)] * 3)

        each_block(body)

    @pl.when(lat > 0)
    def _():
        def body(b, rows):
            mid, at_a, at_b = [read(rows) for read in south]
            for f in range(4):
                far = shift(at_b, 8 * f + 5, 0)
                far = jnp.where(slot_1_lane, shift(at_a, 8 * f + 5, 0), far)
                put_south(b, f, [shift(mid, 8 * f + 5, 0), shift(mid, 8 * f + 4, 0), far])

        each_block(body)

    @pl.when(lat < lat_count - 1)
    def _():
        def body(b, rows):
            mid, at_a, at_b = [read(rows) for read in north]
            for f in range(4):
                far = shift(at_b, 8 * f, 127)
                far = jnp.where(slot_1_lane, shift(at_a, 8 * f, 127), far)
                put_north(b, f, [shift(mid, 8 * f, 127), shift(mid, 8 * f + 1, 127), far])

        each_block(body)

    for top_odd in range(2):

        @pl.when((lat == lat_count - 1) & (odd == top_odd))
        def _(top_odd=top_odd):
            def body(b, rows):
                near, other = folds[0](rows), folds[1 + top_odd](rows)
                if top_odd:
                    near, other = other, near
                for f in range(4):
                    mine = 8 * f + 4 + 2 * (1 - top_odd)
                    beside = 8 * f + 4 + 2 * top_odd
                    values = []
                    for source in (mine + 1, mine, beside + 1):
                        values.append(
                            jnp.where(slot_1_lane, shift(other, source, 1), shift(near, source, 127))
                        )
                    if f >= 2:
                        values = [-v for v in values]
                    put_north(b, f, values)

            each_block(body)


def step_kernel(
    levels,
    lat_count,
    own,
    side_a,
    side_b,
    edges,
    ambient,
    temp_out,
    salt_out,
    zonal_out,
    merid_out,
    statics,
    columns,
    couple,
    state,
    ratio,
    sems,
):
    odd = parity()
    lat = lax.axis_index("lat")
    padded = own.shape[2]
    blocks = padded // ROWS
    lane = lax.broadcasted_iota(jnp.int32, (ROWS, LANES), 1)
    row = lax.broadcasted_iota(jnp.int32, (ROWS, LANES), 0)
    first_lane = lane == 0
    last_lane = lane == LANES - 1
    slot_1_lane = (lane == 1) | (lane == 2)
    south_lane = (lane == 0) | (lane == 2)

    def swap(x):
        return jnp.where(slot_1_lane, pltpu.roll(x, 2, 1), pltpu.roll(x, LANES - 2, 1))

    def to_slot(x, slot):
        return x if slot == 0 else pltpu.roll(x, LANES - 2, 1)

    def northern(x, edge):
        return jnp.where(last_lane, edge, pltpu.roll(x, LANES - 1, 1))

    def southern(x, edge):
        return jnp.where(first_lane, edge, pltpu.roll(x, 1, 1))

    def ring(own_0, own_1):
        return jnp.where(slot_1_lane, pltpu.roll(own_1, 2, 1), own_0)

    def static_row(ref, index, which):
        line = ref[index + (pl.ds(levels + which, 1), slice(None))]
        return jnp.broadcast_to(line, (ROWS, LANES))

    sigma = jnp.where(odd == 0, 1.0, -1.0).astype(jnp.float32)
    sources = {
        "own0": (own, (0, 0)),
        "own1": (own, (1, 0)),
        "near0": (side_b, (0, 0)),
        "near1": (side_a, (1, 0)),
        "far0": (side_b, (1, 0)),
        "far1": (side_a, (0, 0)),
        "rim": (edges, (0, 0)),
        "rim2": (edges, (1, 0)),
        "corner": (edges, (2, 0)),
    }
    held = {name: [static_row(r, i, w) for w in (FLOOD_ROW, MIX_ROW)] for name, (r, i) in sources.items()}

    def neighbours(get, name):
        if name == "rim":
            centre = get("rim")
            beside = ring(get("own0"), get("own1"))
            beyond = get("rim2")
            north_cell = jnp.where(south_lane, beside, beyond)
            south_cell = jnp.where(south_lane, beyond, beside)
            return swap(centre), get("corner"), north_cell, south_cell
        slot = int(name[-1])
        centre = get(name)
        if name.startswith("own"):
            inner, outer, edge = get("own%d" % (1 - slot)), get("near%d" % slot), get("rim")
        else:
            inner, outer, edge = get("own%d" % slot), get("far%d" % slot), get("corner")
        edge = to_slot(edge, slot)
        return inner, outer, northern(centre, edge), southern(centre, edge)

    cell_sets = ("own0", "own1", "near0", "near1", "rim")
    for n, name in enumerate(cell_sets):
        flood_at = neighbours(lambda k: held[k][0], name)
        mix_at = neighbours(lambda k: held[k][1], name)
        statics[n, 0] = held[name][0]
        for m in range(4):
            statics[n, 1 + m] = jnp.minimum(held[name][0], flood_at[m])
            statics[n, 5 + m] = (0.5 * DT) * (held[name][1] + mix_at[m])

    total_rows = LANES * lat_count
    place = lat * LANES + lane
    rim_place = lat * LANES + jnp.where(south_lane, -1, LANES)

    def turning(index):
        index = jnp.where(index >= total_rows, 2 * total_rows - 1 - index, index)
        return DT * (0.2 + index.astype(jnp.float32) / total_rows)

    planet = {True: turning(rim_place), False: turning(place)}
    sigma_of = {
        "own0": sigma,
        "near0": sigma,
        "own1": -sigma,
        "near1": -sigma,
        "rim": jnp.where(slot_1_lane, -sigma, sigma),
    }

    def running(x, carry):
        for step in (1, 2, 4):
            x = x + jnp.where(row >= step, pltpu.roll(x, step, 0), 0.0)
        x = x + carry
        return x, jnp.broadcast_to(x[ROWS - 1 :, :], (ROWS, LANES))

    def advance(name, level, fields, pressure):
        n = cell_sets.index(name)
        wet = level < statics[n, 0]
        weights = [jnp.where(level < statics[n, 1 + m], statics[n, 5 + m], 0.0) for m in range(4)]
        keep = jnp.where(wet, 1.0, 0.0)
        centre = keep - ((weights[0] + weights[1]) + (weights[2] + weights[3]))
        half = jnp.where(wet, 0.5 * DT, 0.0)
        along = half * sigma_of[name]
        flow_u, flow_v = fields[2][name], fields[3][name]
        drift_u = along * flow_u
        drift_v = half * flow_v
        inner, outer, north_w, south_w = (
            weights[0] - drift_u,
            weights[1] + drift_u,
            weights[2] - drift_v,
            weights[3] + drift_v,
        )
        out = []
        for f in range(4):
            cells = neighbours(lambda k, f=f: fields[f][k], name)
            value = centre * fields[f][name]
            value = value + ((inner * cells[0] + outer * cells[1]) + (north_w * cells[2] + south_w * cells[3]))
            out.append(value)
        cells = neighbours(lambda k: pressure[k], name)
        turn = keep * planet[name == "rim"]
        out[2] = out[2] + (turn * flow_v - (0.5 * along) * (cells[0] - cells[1]))
        out[3] = out[3] - (turn * flow_u + (0.5 * half) * (cells[2] - cells[3]))
        return out

    all_sets = ("own0", "own1", "near0", "near1", "far0", "far1", "rim", "rim2", "corner")
    zero = jnp.zeros((ROWS, LANES), jnp.float32)
    ambient_row = [
        jnp.broadcast_to(jnp.where(odd == s, ambient[0:1, :], ambient[1:2, :]), (ROWS, LANES)) for s in range(2)
    ]

    def block_body(b, carry):
        carry_1, carry_2, carry_3 = carry
        rows = pl.ds(pl.multiple_of(ROWS * b, ROWS), ROWS)
        level = (row + ROWS * b).astype(jnp.float32)
        fields = [{k: sources[k][0][sources[k][1][0], f, rows, :] for k in all_sets} for f in range(4)]
        pressure = {}
        next_1 = []
        for k, c in zip(all_sets, carry_1):
            pressure[k], c = running(density(fields[0][k], fields[1][k]), c)
            next_1.append(c)
        updated = {name: advance(name, level, fields, pressure) for name in cell_sets}
        fields = [{name: updated[name][f] for name in cell_sets} for f in range(4)]
        pressure = {}
        next_2 = []
        for k, c in zip(cell_sets, carry_2):
            pressure[k], c = running(density(fields[0][k], fields[1][k]), c)
            next_2.append(c)
        next_3 = []
        for s in range(2):
            final = advance("own%d" % s, level, fields, pressure)
            place_s = odd if s == 0 else 1 - odd
            dense = density(final[0], final[1])
            above = jnp.where(row == 0, carry_3[s], pltpu.roll(dense, 1, 0))
            next_3.append(jnp.broadcast_to(dense[ROWS - 1 :, :], (ROWS, LANES)))
            gate = (level < statics[s, 0]) & (level > 0.0)
            lower = ambient_row[s] * (0.2 + 1.0 / (1.0 + 10.0 * jnp.maximum(dense - above, 0.0)))
            lower = jnp.where(gate, lower, 0.0)
            for f in range(4):
                columns[rows, 2 * f + place_s, :] = final[f]
                couple[rows, 2 * f + place_s, :] = lower
        return tuple(next_1), tuple(next_2), tuple(next_3)

    lax.fori_loop(
        0, blocks, block_body, ((zero,) * len(all_sets), (zero,) * len(cell_sets), (zero,) * 2), unroll=blocks
    )

    top = jnp.ones((ROWS, LANES), jnp.float32)
    bottom = top
    value = zero
    lower = zero
    for k in range(levels):
        upper = couple[k + 1]
        grown = top + upper * bottom
        inverse = bottom / grown
        value = columns[k] * inverse + (lower * inverse) * value
        state[k] = value
        ratio[k] = upper * inverse
        top = grown + upper * top
        bottom = grown
        if k % RESCALE == RESCALE - 1:
            scale = 1.0 / bottom
            top, bottom = top * scale, jnp.ones_like(bottom)
        lower = upper
    current = value
    for k in range(levels - 2, -1, -1):
        current = state[k] + ratio[k] * current
        state[k] = current
    copies = []
    for f, out in enumerate((temp_out, salt_out, zonal_out, merid_out)):
        copy = pltpu.make_async_copy(state.at[:, pl.ds(2 * f, 2), :], out, sems.at[f])
        copy.start()
        copies.append(copy)
    for copy in copies:
        copy.wait()


def pairs_a(count):
    return [(i, i ^ 1) for i in range(count)]


def pairs_b(count, wrap):
    found = []
    for i in range(1, count - 1):
        found.append((i, i + 1 if i % 2 else i - 1))
    if wrap:
        found += [(0, count - 1), (count - 1, 0)]
    return found


def shards(temp, salt, zonal, merid, flood, mix, ambient):
    levels = temp.shape[0]
    lon_count = lax.axis_size("lon")
    lat_count = lax.axis_size("lat")
    axes = ("lon", "lat")
    tile, edge = pack((temp, salt, zonal, merid), flood, mix)
    lon_a, lon_b = pairs_a(lon_count), pairs_b(lon_count, True)

    def joint(lon_pairs, lat_pairs):
        return [
            (i * lat_count + m, j * lat_count + n) for i, j in lon_pairs for m, n in lat_pairs
        ]

    same = [(i, i) for i in range(lon_count)]
    side_b = lax.ppermute(tile, "lon", lon_b)
    side_a = lax.ppermute(tile, "lon", lon_a)
    last = lat_count - 1
    mirror = [(i, lon_count - 1 - i) for i in range(lon_count)]
    mirror_odd = [(i, (lon_count - 2 - i) % lon_count) for i in range(1, lon_count, 2)]
    fold_2 = lax.ppermute(edge, axes, joint(mirror_odd, [(last, last)]))
    same = [(i, i) for i in range(lon_count)]
    rounds = [pairs_a(lat_count)] + ([pairs_b(lat_count, False)] if lat_count > 2 else [])
    fold_1 = lax.ppermute(edge, axes, joint(mirror, [(last, last)]))
    got = []
    for lats in rounds:
        mid = lax.ppermute(edge, axes, joint(same, lats))
        at_b = lax.ppermute(edge, axes, joint(lon_b, lats))
        got.append([mid, lax.ppermute(mid, "lon", lon_a), at_b])
    if len(got) == 1:
        north = south = got[0]
    else:
        flip = lax.rem(lax.axis_index("lat"), 2) == 0
        north = [jnp.where(flip, x, y) for x, y in zip(*got)]
        south = [jnp.where(flip, y, x) for x, y in zip(*got)]
    fold_even = lax.ppermute(fold_1, "lon", lon_a)
    arrays = [fold_2, fold_1, fold_even, south[2], north[2], south[0], north[0], south[1], north[1]]
    padded = tile.shape[2]
    vmem = pl.BlockSpec(memory_space=pltpu.VMEM)
    edges = pl.pallas_call(
        functools.partial(edge_kernel, lat_count),
        out_shape=jax.ShapeDtypeStruct((3, 4, padded, LANES), jnp.float32),
        in_specs=[vmem] * len(arrays),
        out_specs=vmem,
        compiler_params=pltpu.CompilerParams(vmem_limit_bytes=VMEM_LIMIT),
    )(*arrays)
    result = jax.ShapeDtypeStruct(temp.shape, jnp.float32)
    return pl.pallas_call(
        functools.partial(step_kernel, levels, lat_count),
        out_shape=(result,) * 4,
        in_specs=[vmem] * 5,
        out_specs=(pl.BlockSpec(memory_space=pltpu.HBM),) * 4,
        scratch_shapes=[
            pltpu.VMEM((5, 9, ROWS, LANES), jnp.float32),
            pltpu.VMEM((padded, ROWS, LANES), jnp.float32),
            pltpu.VMEM((padded, ROWS, LANES), jnp.float32),
            pltpu.VMEM((levels, ROWS, LANES), jnp.float32),
            pltpu.VMEM((levels, ROWS, LANES), jnp.float32),
            pltpu.SemaphoreType.DMA((4,)),
        ],
        compiler_params=pltpu.CompilerParams(vmem_limit_bytes=VMEM_LIMIT),
    )(tile, side_a, side_b, edges, ambient)


def solution(mesh):
    cube = P(None, "lon", "lat")
    plane = P("lon", "lat")
    return jax.shard_map(
        shards,
        mesh=mesh,
        in_specs=(cube,) * 4 + (plane,) * 3,
        out_specs=(cube,) * 4,
        check_vma=False,
    )
```

```python
import functools

import jax
import jax.numpy as jnp
from jax import lax
from jax.experimental import pallas as pl
from jax.experimental.pallas import tpu as pltpu
from jax.sharding import PartitionSpec as P

SUBSTEPS = 2
DT = 0.05

LANES = 128
VMEM_LIMIT = 16 << 20
SPAN = 32
PER_ROW = LANES // SPAN
WIDEN_COST = 1 << 32
RESCALE = 16
ROWS = 8
FLOOD_ROW = 0
MIX_ROW = 1


def density(temp, salt):
    return temp * (0.03 * salt - 0.05 * temp - 0.2) + 0.8 * salt


def pack_kernel(levels, temp, salt, zonal, merid, flood, mix, tile, edge, flood_here, mix_here, sems):
    copies = [
        pltpu.make_async_copy(flood, flood_here, sems.at[8]),
        pltpu.make_async_copy(mix, mix_here, sems.at[9]),
    ]
    for copy in copies:
        copy.start()
    for f, field in enumerate((temp, salt, zonal, merid)):
        for c in range(2):
            copy = pltpu.make_async_copy(
                field.at[:, c, :], tile.at[c, f, pl.ds(0, levels), :], sems.at[2 * f + c]
            )
            copy.start()
            copies.append(copy)
    padded = tile.shape[2]
    zero = jnp.zeros((padded - levels, LANES), jnp.float32)
    for f in range(4):
        for s in range(2):
            tile[s, f, pl.ds(levels, padded - levels), :] = zero
    for copy in copies[:2]:
        copy.wait()
    for c in range(2):
        tile[c, 0, pl.ds(levels + FLOOD_ROW, 1), :] = flood_here[pl.ds(c, 1), :].astype(jnp.float32)
        tile[c, 0, pl.ds(levels + MIX_ROW, 1), :] = mix_here[pl.ds(c, 1), :]
    lane = lax.broadcasted_iota(jnp.int32, (ROWS, LANES), 1)
    totals = [jnp.zeros((ROWS, LANES), jnp.float32)] * (edge.shape[0] // ROWS)
    for f in range(4):
        for copy in copies[2 + 2 * f : 4 + 2 * f]:
            copy.wait()
        for s in range(2):
            for b in range(padded // ROWS):
                place = SPAN * (b % PER_ROW) + 8 * f + 4 * s
                moved = pltpu.roll(tile[s, f, pl.ds(ROWS * b, ROWS), :], (place + 2) % LANES, 1)
                totals[b // PER_ROW] = jnp.where((lane >> 2) == place // 4, moved, totals[b // PER_ROW])
    for b, total in enumerate(totals):
        edge[pl.ds(ROWS * b, ROWS), :] = total


def compact_rows(padded):
    return -(-padded // (ROWS * PER_ROW)) * ROWS


def pack(fields, flood, mix):
    levels = fields[0].shape[0]
    padded = (levels + 2 + ROWS - 1) // ROWS * ROWS
    return pl.pallas_call(
        functools.partial(pack_kernel, levels),
        out_shape=(
            jax.ShapeDtypeStruct((2, 4, padded, LANES), jnp.float32),
            jax.ShapeDtypeStruct((compact_rows(padded), LANES), jnp.float32),
        ),
        in_specs=[pl.BlockSpec(memory_space=pltpu.HBM)] * 6,
        out_specs=(pl.BlockSpec(memory_space=pltpu.VMEM),) * 2,
        scratch_shapes=[
            pltpu.VMEM(flood.shape, flood.dtype),
            pltpu.VMEM(mix.shape, mix.dtype),
            pltpu.SemaphoreType.DMA((10,)),
        ],
        compiler_params=pltpu.CompilerParams(vmem_limit_bytes=VMEM_LIMIT),
    )(*[pltpu.with_memory_space_constraint(x, pltpu.HBM) for x in (*fields, flood, mix)])


def compact_place(b):
    return pl.ds(ROWS * (b // PER_ROW), ROWS), SPAN * (b % PER_ROW)


def widen_kernel(rounds, blocks, own, west, *messages):
    *messages, own_again = messages
    own_again[...] = own[...]
    lane = lax.broadcasted_iota(jnp.int32, (ROWS, LANES), 1)
    totals = [[jnp.zeros((ROWS, LANES), jnp.float32)] * (own.shape[0] // ROWS) for _ in messages]
    for b in range(blocks):
        rows, start = compact_place(b)
        line = pltpu.roll(own[rows, :], -start % LANES, 1)
        beside = pltpu.roll(west[rows, :], -start % LANES, 1)
        found = []
        for n in range(rounds):
            northward = lax.rem(lax.axis_index("lat") + n, 2) == 0
            pair = jnp.where(northward, line, pltpu.roll(line, LANES - 2, 1))
            corner = jnp.where(northward, pltpu.roll(beside, LANES - 3, 1), pltpu.roll(beside, LANES - 4, 1))
            found.append(jnp.where((lane & 2) == 0, pair, corner))
        found.append(jnp.where((lane & 2) == 0, line, pltpu.roll(beside, 2, 1)))
        for total, values in zip(totals, found):
            moved = pltpu.roll(values, start, 1)
            total[b // PER_ROW] = jnp.where((lane >> 5) == b % PER_ROW, moved, total[b // PER_ROW])
    for message, total in zip(messages, totals):
        for b, values in enumerate(total):
            message[pl.ds(ROWS * b, ROWS), :] = values


def widen(rounds, blocks, edge, west):
    vmem = pl.BlockSpec(memory_space=pltpu.VMEM)
    return pl.pallas_call(
        functools.partial(widen_kernel, rounds, blocks),
        out_shape=(jax.ShapeDtypeStruct(edge.shape, jnp.float32),) * (rounds + 2),
        in_specs=[vmem] * 2,
        out_specs=(vmem,) * (rounds + 2),
        compiler_params=pltpu.CompilerParams(vmem_limit_bytes=VMEM_LIMIT),
        cost_estimate=pl.CostEstimate(flops=WIDEN_COST, bytes_accessed=0, transcendentals=0),
    )(edge, west)


def edge_kernel(lat_count, south_east, north_east, south, north, fold, edges, lines):
    lat = lax.axis_index("lat")
    blocks = edges.shape[2] // ROWS
    lane = lax.broadcasted_iota(jnp.int32, (ROWS, LANES), 1)
    first_slot = (lane & 4) == 0

    def back(x, lanes):
        return pltpu.roll(x, -lanes % LANES, 1)

    def unpacked(ref, b, lanes=0):
        rows, start = compact_place(b)
        return back(ref[rows, :], start + lanes)

    def corners(b, beside, east, lanes):
        return jnp.where(first_slot, unpacked(beside, b, lanes), unpacked(east, b, 2 * lanes - 6))

    def put(b, ones, twos, sides):
        rows = pl.ds(ROWS * b, ROWS)
        below = lat > 0
        cells = jnp.where(below, unpacked(south, b), 0.0)
        beside = jnp.where(below, corners(b, south, south_east, 1), 0.0)
        lines[0, rows, :] = jnp.where((lane & 3) == 1, cells, ones)
        lines[1, rows, :] = jnp.where((lane & 3) == 0, cells, twos)
        lines[2, rows, :] = jnp.where((lane & 3) == 1, beside, sides)

    @pl.when(lat < lat_count - 1)
    def _():
        for b in range(blocks):
            put(b, unpacked(north, b), unpacked(north, b, 2), corners(b, north, north_east, 2))

    @pl.when(lat == lat_count - 1)
    def _():
        turned = jnp.where(lane >= 16, -1.0, 1.0)
        turned_two = jnp.where((lane >= 15) & (lane < LANES - 1), -1.0, 1.0)
        for b in range(blocks):
            near, other = unpacked(fold, b, 1), unpacked(fold, b, 3)
            sides = jnp.where(first_slot, unpacked(fold, b, 5), unpacked(fold, b, -1))
            put(
                b,
                turned * jnp.where(first_slot, near, other),
                turned_two * jnp.where(first_slot, other, near),
                turned * sides,
            )

    for b in range(blocks):
        rows = pl.ds(ROWS * b, ROWS)
        for f in range(4):
            edges[0, f, rows, :] = back(lines[0, rows, :], 8 * f + 1)
            edges[1, f, rows, :] = back(lines[1, rows, :], 8 * f)
            edges[2, f, rows, :] = back(lines[2, rows, :], 8 * f + 1)


def step_kernel(
    levels,
    lat_count,
    own,
    east,
    west,
    edges,
    ambient,
    temp_out,
    salt_out,
    zonal_out,
    merid_out,
    statics,
    columns,
    couple,
    state,
    ratio,
    sems,
):
    lat = lax.axis_index("lat")
    padded = own.shape[2]
    blocks = padded // ROWS
    lane = lax.broadcasted_iota(jnp.int32, (ROWS, LANES), 1)
    row = lax.broadcasted_iota(jnp.int32, (ROWS, LANES), 0)
    first_lane = lane == 0
    last_lane = lane == LANES - 1
    slot_1_lane = (lane == 3) | (lane == 4)
    south_lane = (lane == 0) | (lane == 4)

    def swap(x):
        return jnp.where(slot_1_lane, pltpu.roll(x, 4, 1), pltpu.roll(x, LANES - 4, 1))

    def to_slot(x, slot):
        return x if slot == 0 else pltpu.roll(x, LANES - 4, 1)

    def northern(x, edge):
        return jnp.where(last_lane, edge, pltpu.roll(x, LANES - 1, 1))

    def southern(x, edge):
        return jnp.where(first_lane, edge, pltpu.roll(x, 1, 1))

    def ring(own_0, own_1):
        return jnp.where(slot_1_lane, pltpu.roll(own_1, 4, 1), own_0)

    def static_row(ref, index, which):
        line = ref[index + (pl.ds(levels + which, 1), slice(None))]
        return jnp.broadcast_to(line, (ROWS, LANES))

    sources = {
        "own0": (own, (0, 0)),
        "own1": (own, (1, 0)),
        "near0": (west, (1, 0)),
        "near1": (east, (0, 0)),
        "far0": (west, (0, 0)),
        "far1": (east, (1, 0)),
        "rim": (edges, (0, 0)),
        "rim2": (edges, (1, 0)),
        "corner": (edges, (2, 0)),
    }
    held = {name: [static_row(r, i, w) for w in (FLOOD_ROW, MIX_ROW)] for name, (r, i) in sources.items()}

    def neighbours(get, name):
        if name == "rim":
            centre = get("rim")
            beside = ring(get("own0"), get("own1"))
            beyond = get("rim2")
            north_cell = jnp.where(south_lane, beside, beyond)
            south_cell = jnp.where(south_lane, beyond, beside)
            return swap(centre), get("corner"), north_cell, south_cell
        slot = int(name[-1])
        centre = get(name)
        if name.startswith("own"):
            inner, outer, edge = get("own%d" % (1 - slot)), get("near%d" % slot), get("rim")
        else:
            inner, outer, edge = get("own%d" % slot), get("far%d" % slot), get("corner")
        edge = to_slot(edge, slot)
        return inner, outer, northern(centre, edge), southern(centre, edge)

    cell_sets = ("own0", "own1", "near0", "near1", "rim")
    for n, name in enumerate(cell_sets):
        flood_at = neighbours(lambda k: held[k][0], name)
        mix_at = neighbours(lambda k: held[k][1], name)
        statics[n, 0] = held[name][0]
        for m in range(4):
            statics[n, 1 + m] = jnp.minimum(held[name][0], flood_at[m])
            statics[n, 5 + m] = (0.5 * DT) * (held[name][1] + mix_at[m])

    total_rows = LANES * lat_count
    place = lat * LANES + lane
    rim_place = lat * LANES + jnp.where(south_lane, -1, LANES)

    def turning(index):
        index = jnp.where(index >= total_rows, 2 * total_rows - 1 - index, index)
        return DT * (0.2 + index.astype(jnp.float32) / total_rows)

    planet = {True: turning(rim_place), False: turning(place)}
    sigma_of = {
        "own0": 1.0,
        "near0": 1.0,
        "own1": -1.0,
        "near1": -1.0,
        "rim": jnp.where(slot_1_lane, -1.0, 1.0),
    }

    def running(x, carry):
        for step in (1, 2, 4):
            x = x + jnp.where(row >= step, pltpu.roll(x, step, 0), 0.0)
        x = x + carry
        return x, jnp.broadcast_to(x[ROWS - 1 :, :], (ROWS, LANES))

    def advance(name, level, fields, pressure):
        n = cell_sets.index(name)
        wet = level < statics[n, 0]
        weights = [jnp.where(level < statics[n, 1 + m], statics[n, 5 + m], 0.0) for m in range(4)]
        keep = jnp.where(wet, 1.0, 0.0)
        centre = keep - ((weights[0] + weights[1]) + (weights[2] + weights[3]))
        half = jnp.where(wet, 0.5 * DT, 0.0)
        along = half * sigma_of[name]
        flow_u, flow_v = fields[2][name], fields[3][name]
        drift_u = along * flow_u
        drift_v = half * flow_v
        inner, outer, north_w, south_w = (
            weights[0] - drift_u,
            weights[1] + drift_u,
            weights[2] - drift_v,
            weights[3] + drift_v,
        )
        out = []
        for f in range(4):
            cells = neighbours(lambda k, f=f: fields[f][k], name)
            value = centre * fields[f][name]
            value = value + ((inner * cells[0] + outer * cells[1]) + (north_w * cells[2] + south_w * cells[3]))
            out.append(value)
        cells = neighbours(lambda k: pressure[k], name)
        turn = keep * planet[name == "rim"]
        out[2] = out[2] + (turn * flow_v - (0.5 * along) * (cells[0] - cells[1]))
        out[3] = out[3] - (turn * flow_u + (0.5 * half) * (cells[2] - cells[3]))
        return out

    all_sets = ("own0", "own1", "near0", "near1", "far0", "far1", "rim", "rim2", "corner")
    zero = jnp.zeros((ROWS, LANES), jnp.float32)
    ambient_row = [
        jnp.broadcast_to(ambient[s : s + 1, :], (ROWS, LANES)) for s in range(2)
    ]

    def block_body(b, carry):
        carry_1, carry_2, carry_3 = carry
        rows = pl.ds(pl.multiple_of(ROWS * b, ROWS), ROWS)
        level = (row + ROWS * b).astype(jnp.float32)
        fields = [{k: sources[k][0][sources[k][1][0], f, rows, :] for k in all_sets} for f in range(4)]
        pressure = {}
        next_1 = []
        for k, c in zip(all_sets, carry_1):
            pressure[k], c = running(density(fields[0][k], fields[1][k]), c)
            next_1.append(c)
        updated = {name: advance(name, level, fields, pressure) for name in cell_sets}
        fields = [{name: updated[name][f] for name in cell_sets} for f in range(4)]
        pressure = {}
        next_2 = []
        for k, c in zip(cell_sets, carry_2):
            pressure[k], c = running(density(fields[0][k], fields[1][k]), c)
            next_2.append(c)
        next_3 = []
        for s in range(2):
            final = advance("own%d" % s, level, fields, pressure)
            dense = density(final[0], final[1])
            above = jnp.where(row == 0, carry_3[s], pltpu.roll(dense, 1, 0))
            next_3.append(jnp.broadcast_to(dense[ROWS - 1 :, :], (ROWS, LANES)))
            gate = (level < statics[s, 0]) & (level > 0.0)
            lower = ambient_row[s] * (0.2 + 1.0 / (1.0 + 10.0 * jnp.maximum(dense - above, 0.0)))
            lower = jnp.where(gate, lower, 0.0)
            for f in range(4):
                columns[rows, 2 * f + s, :] = final[f]
                couple[rows, 2 * f + s, :] = lower
        return tuple(next_1), tuple(next_2), tuple(next_3)

    lax.fori_loop(
        0, blocks, block_body, ((zero,) * len(all_sets), (zero,) * len(cell_sets), (zero,) * 2), unroll=blocks
    )

    top = jnp.ones((ROWS, LANES), jnp.float32)
    bottom = top
    value = zero
    lower = zero
    for k in range(levels):
        upper = couple[k + 1]
        grown = top + upper * bottom
        inverse = bottom / grown
        value = columns[k] * inverse + (lower * inverse) * value
        state[k] = value
        ratio[k] = upper * inverse
        top = grown + upper * top
        bottom = grown
        if k % RESCALE == RESCALE - 1:
            scale = 1.0 / bottom
            top, bottom = top * scale, jnp.ones_like(bottom)
        lower = upper
    current = value
    copies = []

    def send(start, stop, group):
        for f, out in enumerate((temp_out, salt_out, zonal_out, merid_out)):
            part = pl.ds(start, stop - start)
            copy = pltpu.make_async_copy(state.at[part, pl.ds(2 * f, 2), :], out.at[part], sems.at[4 * group + f])
            copy.start()
            copies.append(copy)

    half = levels // 2
    for k in range(levels - 2, -1, -1):
        current = state[k] + ratio[k] * current
        state[k] = current
        if k == half:
            send(half, levels, 0)
    send(0, half, 1)
    for copy in copies:
        copy.wait()


def lat_rounds(count):
    rounds = [[(i, i ^ 1) for i in range(count) if i ^ 1 < count]]
    if count > 2:
        rounds.append([(i, j) for i in range(1, count) for j in [i + 1 if i % 2 else i - 1] if j < count])
    return rounds


def shards(temp, salt, zonal, merid, flood, mix, ambient):
    levels = temp.shape[0]
    lon_count = lax.axis_size("lon")
    lat_count = lax.axis_size("lat")
    axes = ("lon", "lat")
    tile, edge = pack((temp, salt, zonal, merid), flood, mix)
    def joint(lon_pairs, lat_pairs):
        return [
            (i * lat_count + m, j * lat_count + n) for i, j in lon_pairs for m, n in lat_pairs
        ]

    same = [(i, i) for i in range(lon_count)]
    around = [(0, lon_count - 1), (lon_count - 1, 0)]
    eastward = [(i, (i + 1) % lon_count) for i in range(lon_count)]
    westward = [(j, i) for i, j in eastward]
    same = [(i, i) for i in range(lon_count)]
    mirror = [(i, lon_count - 1 - i) for i in range(lon_count)]
    edge_west = lax.ppermute(edge, "lon", eastward)
    west = lax.ppermute(tile, "lon", eastward)
    east = lax.ppermute(tile, "lon", westward)
    rounds = lat_rounds(lat_count)
    *bands, top_edge, edge = widen(len(rounds), tile.shape[2] // ROWS, edge, edge_west)
    got = [
        (lax.ppermute(band, axes, joint(same, lats)), lax.ppermute(edge, axes, joint(westward, lats)))
        for band, lats in zip(bands, rounds)
    ]
    chip = [(i, i ^ 1) for i in range(lon_count)]
    pairs = joint(mirror, [(lat_count - 1, lat_count - 1)]) + joint(chip, [(i, i) for i in range(lat_count - 1)])
    fold = lax.ppermute(top_edge, axes, pairs)
    if len(got) == 1:
        south = north = got[0]
    else:
        flip = lax.rem(lax.axis_index("lat"), 2) == 0
        north = [jnp.where(flip, x, y) for x, y in zip(*got)]
        south = [jnp.where(flip, y, x) for x, y in zip(*got)]
    padded = tile.shape[2]
    vmem = pl.BlockSpec(memory_space=pltpu.VMEM)
    edges = pl.pallas_call(
        functools.partial(edge_kernel, lat_count),
        out_shape=jax.ShapeDtypeStruct((3, 4, padded, LANES), jnp.float32),
        in_specs=[vmem] * 5,
        out_specs=vmem,
        scratch_shapes=[pltpu.VMEM((3, padded, LANES), jnp.float32)],
        compiler_params=pltpu.CompilerParams(vmem_limit_bytes=VMEM_LIMIT),
    )(south[1], north[1], south[0], north[0], fold)
    result = jax.ShapeDtypeStruct(temp.shape, jnp.float32)
    return pl.pallas_call(
        functools.partial(step_kernel, levels, lat_count),
        out_shape=(result,) * 4,
        in_specs=[vmem] * 5,
        out_specs=(pl.BlockSpec(memory_space=pltpu.HBM),) * 4,
        scratch_shapes=[
            pltpu.VMEM((5, 9, ROWS, LANES), jnp.float32),
            pltpu.VMEM((padded, ROWS, LANES), jnp.float32),
            pltpu.VMEM((padded, ROWS, LANES), jnp.float32),
            pltpu.VMEM((levels, ROWS, LANES), jnp.float32),
            pltpu.VMEM((levels, ROWS, LANES), jnp.float32),
            pltpu.SemaphoreType.DMA((8,)),
        ],
        compiler_params=pltpu.CompilerParams(vmem_limit_bytes=VMEM_LIMIT),
    )(tile, east, west, edges, ambient)


def solution(mesh):
    cube = P(None, "lon", "lat")
    plane = P("lon", "lat")
    return jax.shard_map(
        shards,
        mesh=mesh,
        in_specs=(cube,) * 4 + (plane,) * 3,
        out_specs=(cube,) * 4,
        check_vma=False,
    )
```

```python
import functools
import types

import jax
import jax.numpy as jnp
from jax import lax
from jax.experimental import pallas as pl
from jax.experimental.pallas import tpu as pltpu
from jax.sharding import PartitionSpec as P

SUBSTEPS = 2
DT = 0.05

LANES = 128
VMEM_LIMIT = 16 << 20
SPAN = 32
PER_ROW = LANES // SPAN
INNER_COST = 1 << 30
WIDEN_COST = 1 << 32
RESCALE = 16
ROWS = 8
FLOOD_ROW = 0
MIX_ROW = 1


def density(temp, salt):
    return temp * (0.03 * salt - 0.05 * temp - 0.2) + 0.8 * salt


def pack_kernel(levels, temp, salt, zonal, merid, flood, mix, ambient, tile, edge, ambient_here, flood_here, mix_here, sems):
    copies = [
        pltpu.make_async_copy(flood, flood_here, sems.at[8]),
        pltpu.make_async_copy(mix, mix_here, sems.at[9]),
    ]
    for copy in copies:
        copy.start()
    for f, field in enumerate((temp, salt, zonal, merid)):
        for c in range(2):
            copy = pltpu.make_async_copy(
                field.at[:, c, :], tile.at[c, f, pl.ds(0, levels), :], sems.at[2 * f + c]
            )
            copy.start()
            copies.append(copy)
    last_copy = pltpu.make_async_copy(ambient, ambient_here, sems.at[10])
    last_copy.start()
    padded = tile.shape[2]
    zero = jnp.zeros((padded - levels, LANES), jnp.float32)
    for f in range(4):
        for s in range(2):
            tile[s, f, pl.ds(levels, padded - levels), :] = zero
    for copy in copies[:2]:
        copy.wait()
    for c in range(2):
        tile[c, 0, pl.ds(levels + FLOOD_ROW, 1), :] = flood_here[pl.ds(c, 1), :].astype(jnp.float32)
        tile[c, 0, pl.ds(levels + MIX_ROW, 1), :] = mix_here[pl.ds(c, 1), :]
    lane = lax.broadcasted_iota(jnp.int32, (ROWS, LANES), 1)
    totals = [jnp.zeros((ROWS, LANES), jnp.float32)] * (edge.shape[0] // ROWS)
    for f in range(4):
        for copy in copies[2 + 2 * f : 4 + 2 * f]:
            copy.wait()
        for s in range(2):
            for b in range(padded // ROWS):
                place = SPAN * (b % PER_ROW) + 8 * f + 4 * s
                moved = pltpu.roll(tile[s, f, pl.ds(ROWS * b, ROWS), :], (place + 2) % LANES, 1)
                totals[b // PER_ROW] = jnp.where((lane >> 2) == place // 4, moved, totals[b // PER_ROW])
    for b, total in enumerate(totals):
        edge[pl.ds(ROWS * b, ROWS), :] = total
    last_copy.wait()


def compact_rows(padded):
    return -(-padded // (ROWS * PER_ROW)) * ROWS


def pack(fields, flood, mix, ambient):
    levels = fields[0].shape[0]
    padded = (levels + 2 + ROWS - 1) // ROWS * ROWS
    return pl.pallas_call(
        functools.partial(pack_kernel, levels),
        out_shape=(
            jax.ShapeDtypeStruct((2, 4, padded, LANES), jnp.float32),
            jax.ShapeDtypeStruct((compact_rows(padded), LANES), jnp.float32),
            jax.ShapeDtypeStruct(ambient.shape, jnp.float32),
        ),
        in_specs=[pl.BlockSpec(memory_space=pltpu.HBM)] * 7,
        out_specs=(pl.BlockSpec(memory_space=pltpu.VMEM),) * 3,
        scratch_shapes=[
            pltpu.VMEM(flood.shape, flood.dtype),
            pltpu.VMEM(mix.shape, mix.dtype),
            pltpu.SemaphoreType.DMA((11,)),
        ],
        compiler_params=pltpu.CompilerParams(vmem_limit_bytes=VMEM_LIMIT),
    )(*[pltpu.with_memory_space_constraint(x, pltpu.HBM) for x in (*fields, flood, mix, ambient)])


def compact_place(b):
    return pl.ds(ROWS * (b // PER_ROW), ROWS), SPAN * (b % PER_ROW)


def widen_kernel(rounds, blocks, own, west, *messages):
    *messages, own_again = messages
    own_again[...] = own[...]
    lane = lax.broadcasted_iota(jnp.int32, (ROWS, LANES), 1)
    totals = [[jnp.zeros((ROWS, LANES), jnp.float32)] * (own.shape[0] // ROWS) for _ in messages]
    for b in range(blocks):
        rows, start = compact_place(b)
        line = pltpu.roll(own[rows, :], -start % LANES, 1)
        beside = pltpu.roll(west[rows, :], -start % LANES, 1)
        found = []
        for n in range(rounds):
            northward = lax.rem(lax.axis_index("lat") + n, 2) == 0
            pair = jnp.where(northward, line, pltpu.roll(line, LANES - 2, 1))
            corner = jnp.where(northward, pltpu.roll(beside, LANES - 3, 1), pltpu.roll(beside, LANES - 4, 1))
            found.append(jnp.where((lane & 2) == 0, pair, corner))
        found.append(jnp.where((lane & 2) == 0, line, pltpu.roll(beside, 2, 1)))
        for total, values in zip(totals, found):
            moved = pltpu.roll(values, start, 1)
            total[b // PER_ROW] = jnp.where((lane >> 5) == b % PER_ROW, moved, total[b // PER_ROW])
    for message, total in zip(messages, totals):
        for b, values in enumerate(total):
            message[pl.ds(ROWS * b, ROWS), :] = values


def widen(rounds, blocks, edge, west):
    vmem = pl.BlockSpec(memory_space=pltpu.VMEM)
    return pl.pallas_call(
        functools.partial(widen_kernel, rounds, blocks),
        out_shape=(jax.ShapeDtypeStruct(edge.shape, jnp.float32),) * (rounds + 2),
        in_specs=[vmem] * 2,
        out_specs=(vmem,) * (rounds + 2),
        compiler_params=pltpu.CompilerParams(vmem_limit_bytes=VMEM_LIMIT),
        cost_estimate=pl.CostEstimate(flops=WIDEN_COST, bytes_accessed=0, transcendentals=0),
    )(edge, west)


def edge_kernel(lat_count, south_east, north_east, south, north, fold, _, edges, lines):
    lat = lax.axis_index("lat")
    blocks = edges.shape[2] // ROWS
    lane = lax.broadcasted_iota(jnp.int32, (ROWS, LANES), 1)
    first_slot = (lane & 4) == 0

    def back(x, lanes):
        return pltpu.roll(x, -lanes % LANES, 1)

    def unpacked(ref, b, lanes=0):
        rows, start = compact_place(b)
        return back(ref[rows, :], start + lanes)

    def corners(b, beside, east, lanes):
        return jnp.where(first_slot, unpacked(beside, b, lanes), unpacked(east, b, 2 * lanes - 6))

    def put(b, ones, twos, sides):
        rows = pl.ds(ROWS * b, ROWS)
        below = lat > 0
        cells = jnp.where(below, unpacked(south, b), 0.0)
        beside = jnp.where(below, corners(b, south, south_east, 1), 0.0)
        lines[0, rows, :] = jnp.where((lane & 3) == 1, cells, ones)
        lines[1, rows, :] = jnp.where((lane & 3) == 0, cells, twos)
        lines[2, rows, :] = jnp.where((lane & 3) == 1, beside, sides)

    @pl.when(lat < lat_count - 1)
    def _():
        for b in range(blocks):
            put(b, unpacked(north, b), unpacked(north, b, 2), corners(b, north, north_east, 2))

    @pl.when(lat == lat_count - 1)
    def _():
        turned = jnp.where(lane >= 16, -1.0, 1.0)
        turned_two = jnp.where((lane >= 15) & (lane < LANES - 1), -1.0, 1.0)
        for b in range(blocks):
            near, other = unpacked(fold, b, 1), unpacked(fold, b, 3)
            sides = jnp.where(first_slot, unpacked(fold, b, 5), unpacked(fold, b, -1))
            put(
                b,
                turned * jnp.where(first_slot, near, other),
                turned_two * jnp.where(first_slot, other, near),
                turned * sides,
            )

    for b in range(blocks):
        rows = pl.ds(ROWS * b, ROWS)
        for f in range(4):
            edges[0, f, rows, :] = back(lines[0, rows, :], 8 * f + 1)
            edges[1, f, rows, :] = back(lines[1, rows, :], 8 * f)
            edges[2, f, rows, :] = back(lines[2, rows, :], 8 * f + 1)


def stencil(levels, lat_count, statics):
    lat = lax.axis_index("lat")
    lane = lax.broadcasted_iota(jnp.int32, (ROWS, LANES), 1)
    row = lax.broadcasted_iota(jnp.int32, (ROWS, LANES), 0)
    first_lane = lane == 0
    last_lane = lane == LANES - 1
    slot_1_lane = (lane == 3) | (lane == 4)
    south_lane = (lane == 0) | (lane == 4)

    def swap(x):
        return jnp.where(slot_1_lane, pltpu.roll(x, 4, 1), pltpu.roll(x, LANES - 4, 1))

    def to_slot(x, slot):
        return x if slot == 0 else pltpu.roll(x, LANES - 4, 1)

    def northern(x, edge):
        return jnp.where(last_lane, edge, pltpu.roll(x, LANES - 1, 1))

    def southern(x, edge):
        return jnp.where(first_lane, edge, pltpu.roll(x, 1, 1))

    def ring(own_0, own_1):
        return jnp.where(slot_1_lane, pltpu.roll(own_1, 4, 1), own_0)

    def static_row(ref, index, which):
        line = ref[index + (pl.ds(levels + which, 1), slice(None))]
        return jnp.broadcast_to(line, (ROWS, LANES))

    def neighbours(get, name):
        if name == "rim":
            centre = get("rim")
            beside = ring(get("own0"), get("own1"))
            beyond = get("rim2")
            north_cell = jnp.where(south_lane, beside, beyond)
            south_cell = jnp.where(south_lane, beyond, beside)
            return swap(centre), get("corner"), north_cell, south_cell
        slot = int(name[-1])
        centre = get(name)
        if name.startswith("own"):
            inner, outer, edge = get("own%d" % (1 - slot)), get("near%d" % slot), get("rim")
        else:
            inner, outer, edge = get("own%d" % slot), get("far%d" % slot), get("corner")
        edge = to_slot(edge, slot)
        return inner, outer, northern(centre, edge), southern(centre, edge)

    cell_sets = ("own0", "own1", "near0", "near1", "rim")

    def hold(held, names):
        for name in names:
            n = cell_sets.index(name)
            flood_at = neighbours(lambda k: held[k][0], name)
            mix_at = neighbours(lambda k: held[k][1], name)
            statics[n, 0] = held[name][0]
            for m in range(4):
                statics[n, 1 + m] = jnp.minimum(held[name][0], flood_at[m])
                statics[n, 5 + m] = (0.5 * DT) * (held[name][1] + mix_at[m])

    total_rows = LANES * lat_count
    place = lat * LANES + lane
    rim_place = lat * LANES + jnp.where(south_lane, -1, LANES)

    def turning(index):
        index = jnp.where(index >= total_rows, 2 * total_rows - 1 - index, index)
        return DT * (0.2 + index.astype(jnp.float32) / total_rows)

    planet = {True: turning(rim_place), False: turning(place)}
    sigma_of = {
        "own0": 1.0,
        "near0": 1.0,
        "own1": -1.0,
        "near1": -1.0,
        "rim": jnp.where(slot_1_lane, -1.0, 1.0),
    }

    def running(x, carry):
        for step in (1, 2, 4):
            x = x + jnp.where(row >= step, pltpu.roll(x, step, 0), 0.0)
        x = x + carry
        return x, jnp.broadcast_to(x[ROWS - 1 :, :], (ROWS, LANES))

    def advance(name, level, fields, pressure):
        n = cell_sets.index(name)
        wet = level < statics[n, 0]
        weights = [jnp.where(level < statics[n, 1 + m], statics[n, 5 + m], 0.0) for m in range(4)]
        keep = jnp.where(wet, 1.0, 0.0)
        centre = keep - ((weights[0] + weights[1]) + (weights[2] + weights[3]))
        half = jnp.where(wet, 0.5 * DT, 0.0)
        along = half * sigma_of[name]
        flow_u, flow_v = fields[2][name], fields[3][name]
        drift_u = along * flow_u
        drift_v = half * flow_v
        inner, outer, north_w, south_w = (
            weights[0] - drift_u,
            weights[1] + drift_u,
            weights[2] - drift_v,
            weights[3] + drift_v,
        )
        out = []
        for f in range(4):
            cells = neighbours(lambda k, f=f: fields[f][k], name)
            value = centre * fields[f][name]
            value = value + ((inner * cells[0] + outer * cells[1]) + (north_w * cells[2] + south_w * cells[3]))
            out.append(value)
        cells = neighbours(lambda k: pressure[k], name)
        turn = keep * planet[name == "rim"]
        out[2] = out[2] + (turn * flow_v - (0.5 * along) * (cells[0] - cells[1]))
        out[3] = out[3] - (turn * flow_u + (0.5 * half) * (cells[2] - cells[3]))
        return out

    def whole(sources):
        return {name: [static_row(r, i, w) for w in (FLOOD_ROW, MIX_ROW)] for name, (r, i) in sources.items()}

    turn_lane = jnp.where(last_lane, -1.0, jnp.where(first_lane, 1.0, 0.0))
    return types.SimpleNamespace(
        row=row, cell_sets=cell_sets, to_slot=to_slot, running=running, advance=advance, hold=hold, whole=whole, turn_lane=turn_lane
    )


def tile_sources(own, east, west):
    return {
        "own0": (own, (0, 0)),
        "own1": (own, (1, 0)),
        "near0": (west, (1, 0)),
        "near1": (east, (0, 0)),
        "far0": (west, (0, 0)),
        "far1": (east, (1, 0)),
    }


def inner_kernel(levels, lat_count, own, east, west, partial, pressure_out, statics):
    use = stencil(levels, lat_count, statics)
    blocks = own.shape[2] // ROWS
    zero = jnp.zeros((ROWS, LANES), jnp.float32)
    beyond = {"rim": zero, "corner": zero}
    sources = tile_sources(own, east, west)
    held = use.whole(sources)
    held.update({name: (zero, zero) for name in beyond})
    names = use.cell_sets[:4]
    use.hold(held, names)
    carry = {name: zero for name in sources}
    for b in range(blocks):
        rows = pl.ds(ROWS * b, ROWS)
        level = (use.row + ROWS * b).astype(jnp.float32)
        fields = [{k: r[i[0], f, rows, :] for k, (r, i) in sources.items()} | beyond for f in range(4)]
        pressure = dict(beyond)
        for k in sources:
            pressure[k], carry[k] = use.running(density(fields[0][k], fields[1][k]), carry[k])
        for s in range(2):
            pressure_out[s, rows, :] = pressure["own%d" % s]
        for n, name in enumerate(names):
            for f, value in enumerate(use.advance(name, level, fields, pressure)):
                partial[n, f, rows, :] = value


def step_kernel(
    levels,
    lat_count,
    own,
    east,
    west,
    partial,
    own_pressure,
    edges,
    ambient,
    temp_out,
    salt_out,
    zonal_out,
    merid_out,
    statics,
    ends,
    columns,
    couple,
    state,
    ratio,
    sems,
):
    use = stencil(levels, lat_count, statics)
    row, cell_sets, running = use.row, use.cell_sets, use.running
    blocks = own.shape[2] // ROWS
    zero = jnp.zeros((ROWS, LANES), jnp.float32)
    sources = tile_sources(own, east, west)
    sources.update({"rim": (edges, (0, 0)), "rim2": (edges, (1, 0)), "corner": (edges, (2, 0))})
    held = use.whole(sources)
    use.hold(held, ("own0", "own1", "rim"))
    names = cell_sets[:4]
    edge_of = ("rim", "rim", "corner", "corner")
    at_end = use.turn_lane != 0.0
    for n, name in enumerate(names):
        flood, mix = [use.to_slot(x, n % 2) for x in held[edge_of[n]]]
        ends[n, 0] = held[name][0]
        ends[n, 1] = jnp.where(at_end, jnp.minimum(held[name][0], flood), 0.0)
        ends[n, 2] = (0.5 * DT) * (held[name][1] + mix)
    half_turn = (0.5 * DT) * use.turn_lane
    ambient_row = [jnp.broadcast_to(ambient[s : s + 1, :], (ROWS, LANES)) for s in range(2)]
    rim_sets = ("rim", "rim2", "corner")

    def block_body(b, carry):
        carry_1, carry_2, carry_3 = carry
        rows = pl.ds(pl.multiple_of(ROWS * b, ROWS), ROWS)
        level = (row + ROWS * b).astype(jnp.float32)
        fields = [{k: sources[k][0][sources[k][1][0], f, rows, :] for k in names + rim_sets} for f in range(4)]
        pressure = {"own%d" % s: own_pressure[s, rows, :] for s in range(2)}
        next_1 = []
        for k, c in zip(rim_sets, carry_1):
            pressure[k], c = running(density(fields[0][k], fields[1][k]), c)
            next_1.append(c)
        updated = {"rim": use.advance("rim", level, fields, pressure)}
        for n, name in enumerate(names):
            weight = jnp.where(level < ends[n, 1], ends[n, 2], 0.0)
            half = jnp.where(level < ends[n, 0], half_turn, 0.0)
            reach = weight + half * fields[3][name]
            out = []
            for f in range(4):
                beyond = use.to_slot(fields[f][edge_of[n]], n % 2)
                out.append(partial[n, f, rows, :] + (reach * beyond - weight * fields[f][name]))
            out[3] = out[3] + (0.5 * half) * use.to_slot(pressure[edge_of[n]], n % 2)
            updated[name] = out
        fields = [{name: updated[name][f] for name in cell_sets} for f in range(4)]
        pressure = {}
        next_2 = []
        for k, c in zip(cell_sets, carry_2):
            pressure[k], c = running(density(fields[0][k], fields[1][k]), c)
            next_2.append(c)
        next_3 = []
        for s in range(2):
            final = use.advance("own%d" % s, level, fields, pressure)
            dense = density(final[0], final[1])
            above = jnp.where(row == 0, carry_3[s], pltpu.roll(dense, 1, 0))
            next_3.append(jnp.broadcast_to(dense[ROWS - 1 :, :], (ROWS, LANES)))
            gate = (level < statics[s, 0]) & (level > 0.0)
            lower = ambient_row[s] * (0.2 + 1.0 / (1.0 + 10.0 * jnp.maximum(dense - above, 0.0)))
            lower = jnp.where(gate, lower, 0.0)
            for f in range(4):
                columns[rows, 2 * f + s, :] = final[f]
                couple[rows, 2 * f + s, :] = lower
        return tuple(next_1), tuple(next_2), tuple(next_3)

    lax.fori_loop(
        0, blocks, block_body, ((zero,) * len(rim_sets), (zero,) * len(cell_sets), (zero,) * 2), unroll=blocks
    )

    top = jnp.ones((ROWS, LANES), jnp.float32)
    bottom = top
    value = zero
    lower = zero
    for k in range(levels):
        upper = couple[k + 1]
        grown = top + upper * bottom
        inverse = bottom / grown
        value = columns[k] * inverse + (lower * inverse) * value
        state[k] = value
        ratio[k] = upper * inverse
        top = grown + upper * top
        bottom = grown
        if k % RESCALE == RESCALE - 1:
            scale = 1.0 / bottom
            top, bottom = top * scale, jnp.ones_like(bottom)
        lower = upper
    current = value
    copies = []

    def send(start, stop, group):
        for f, out in enumerate((temp_out, salt_out, zonal_out, merid_out)):
            part = pl.ds(start, stop - start)
            copy = pltpu.make_async_copy(state.at[part, pl.ds(2 * f, 2), :], out.at[part], sems.at[4 * group + f])
            copy.start()
            copies.append(copy)

    half = levels // 2
    for k in range(levels - 2, -1, -1):
        current = state[k] + ratio[k] * current
        state[k] = current
        if k == half:
            send(half, levels, 0)
    send(0, half, 1)
    for copy in copies:
        copy.wait()


def lat_rounds(count):
    rounds = [[(i, i ^ 1) for i in range(count) if i ^ 1 < count]]
    if count > 2:
        rounds.append([(i, j) for i in range(1, count) for j in [i + 1 if i % 2 else i - 1] if j < count])
    return rounds


def shards(temp, salt, zonal, merid, flood, mix, ambient):
    levels = temp.shape[0]
    lon_count = lax.axis_size("lon")
    lat_count = lax.axis_size("lat")
    axes = ("lon", "lat")
    tile, edge, ambient = pack((temp, salt, zonal, merid), flood, mix, ambient)
    def joint(lon_pairs, lat_pairs):
        return [
            (i * lat_count + m, j * lat_count + n) for i, j in lon_pairs for m, n in lat_pairs
        ]

    same = [(i, i) for i in range(lon_count)]
    around = [(0, lon_count - 1), (lon_count - 1, 0)]
    eastward = [(i, (i + 1) % lon_count) for i in range(lon_count)]
    westward = [(j, i) for i, j in eastward]
    same = [(i, i) for i in range(lon_count)]
    mirror = [(i, lon_count - 1 - i) for i in range(lon_count)]
    edge_west = lax.ppermute(edge, "lon", eastward)
    west = lax.ppermute(tile, "lon", eastward)
    east = lax.ppermute(tile, "lon", westward)
    rounds = lat_rounds(lat_count)
    *bands, top_edge, edge = widen(len(rounds), tile.shape[2] // ROWS, edge, edge_west)
    got = [
        (lax.ppermute(band, axes, joint(same, lats)), lax.ppermute(edge, axes, joint(westward, lats)))
        for band, lats in zip(bands, rounds)
    ]
    chip = [(i, i ^ 1) for i in range(lon_count)]
    pairs = joint(mirror, [(lat_count - 1, lat_count - 1)]) + joint(chip, [(i, i) for i in range(lat_count - 1)])
    fold = lax.ppermute(top_edge, axes, pairs)
    if len(got) == 1:
        south = north = got[0]
    else:
        flip = lax.rem(lax.axis_index("lat"), 2) == 0
        north = [jnp.where(flip, x, y) for x, y in zip(*got)]
        south = [jnp.where(flip, y, x) for x, y in zip(*got)]
    padded = tile.shape[2]
    vmem = pl.BlockSpec(memory_space=pltpu.VMEM)
    partial, own_pressure = pl.pallas_call(
        functools.partial(inner_kernel, levels, lat_count),
        out_shape=(
            jax.ShapeDtypeStruct((4, 4, padded, LANES), jnp.float32),
            jax.ShapeDtypeStruct((2, padded, LANES), jnp.float32),
        ),
        in_specs=[vmem] * 3,
        out_specs=(vmem, vmem),
        scratch_shapes=[pltpu.VMEM((5, 9, ROWS, LANES), jnp.float32)],
        compiler_params=pltpu.CompilerParams(vmem_limit_bytes=VMEM_LIMIT),
        cost_estimate=pl.CostEstimate(flops=INNER_COST, bytes_accessed=0, transcendentals=0),
    )(tile, east, west)
    edges = pl.pallas_call(
        functools.partial(edge_kernel, lat_count),
        out_shape=jax.ShapeDtypeStruct((3, 4, padded, LANES), jnp.float32),
        in_specs=[vmem] * 5 + [pl.BlockSpec(memory_space=pl.ANY)],
        out_specs=vmem,
        scratch_shapes=[pltpu.VMEM((3, padded, LANES), jnp.float32)],
        compiler_params=pltpu.CompilerParams(vmem_limit_bytes=VMEM_LIMIT),
    )(south[1], north[1], south[0], north[0], fold, own_pressure)
    result = jax.ShapeDtypeStruct(temp.shape, jnp.float32)
    return pl.pallas_call(
        functools.partial(step_kernel, levels, lat_count),
        out_shape=(result,) * 4,
        in_specs=[vmem] * 7,
        out_specs=(pl.BlockSpec(memory_space=pltpu.HBM),) * 4,
        scratch_shapes=[
            pltpu.VMEM((5, 9, ROWS, LANES), jnp.float32),
            pltpu.VMEM((4, 3, ROWS, LANES), jnp.float32),
            pltpu.VMEM((padded, ROWS, LANES), jnp.float32),
            pltpu.VMEM((padded, ROWS, LANES), jnp.float32),
            pltpu.VMEM((levels, ROWS, LANES), jnp.float32),
            pltpu.VMEM((levels, ROWS, LANES), jnp.float32),
            pltpu.SemaphoreType.DMA((8,)),
        ],
        compiler_params=pltpu.CompilerParams(vmem_limit_bytes=VMEM_LIMIT),
    )(tile, east, west, partial, own_pressure, edges, ambient)


def solution(mesh):
    cube = P(None, "lon", "lat")
    plane = P("lon", "lat")
    return jax.shard_map(
        shards,
        mesh=mesh,
        in_specs=(cube,) * 4 + (plane,) * 3,
        out_specs=(cube,) * 4,
        check_vma=False,
    )
```

```python
import functools
import types

import jax
import jax.numpy as jnp
from jax import lax
from jax.experimental import pallas as pl
from jax.experimental.pallas import tpu as pltpu
from jax.sharding import PartitionSpec as P

SUBSTEPS = 2
DT = 0.05

LANES = 128
VMEM_LIMIT = 16 << 20
SPAN = 32
PER_ROW = LANES // SPAN
INNER_COST = 1 << 30
WIDEN_COST = 1 << 32
RESCALE = 16
ROWS = 8
FLOOD_ROW = 0
MIX_ROW = 1


def density(temp, salt):
    return temp * (0.03 * salt - 0.05 * temp - 0.2) + 0.8 * salt


def pack_kernel(levels, temp, salt, zonal, merid, flood, mix, ambient, tile, edge, ambient_here, flood_here, mix_here, sems):
    copies = [
        pltpu.make_async_copy(flood, flood_here, sems.at[8]),
        pltpu.make_async_copy(mix, mix_here, sems.at[9]),
    ]
    for copy in copies:
        copy.start()
    for f, field in enumerate((temp, salt, zonal, merid)):
        for c in range(2):
            copy = pltpu.make_async_copy(
                field.at[:, c, :], tile.at[c, f, pl.ds(0, levels), :], sems.at[2 * f + c]
            )
            copy.start()
            copies.append(copy)
    last_copy = pltpu.make_async_copy(ambient, ambient_here, sems.at[10])
    last_copy.start()
    padded = tile.shape[2]
    zero = jnp.zeros((padded - levels, LANES), jnp.float32)
    for f in range(4):
        for s in range(2):
            tile[s, f, pl.ds(levels, padded - levels), :] = zero
    for copy in copies[:2]:
        copy.wait()
    for c in range(2):
        tile[c, 0, pl.ds(levels + FLOOD_ROW, 1), :] = flood_here[pl.ds(c, 1), :].astype(jnp.float32)
        tile[c, 0, pl.ds(levels + MIX_ROW, 1), :] = mix_here[pl.ds(c, 1), :]
    lane = lax.broadcasted_iota(jnp.int32, (ROWS, LANES), 1)
    totals = [jnp.zeros((ROWS, LANES), jnp.float32)] * (edge.shape[0] // ROWS)
    for f in range(4):
        for copy in copies[2 + 2 * f : 4 + 2 * f]:
            copy.wait()
        for s in range(2):
            for b in range(padded // ROWS):
                place = SPAN * (b % PER_ROW) + 8 * f + 4 * s
                moved = pltpu.roll(tile[s, f, pl.ds(ROWS * b, ROWS), :], (place + 2) % LANES, 1)
                totals[b // PER_ROW] = jnp.where((lane >> 2) == place // 4, moved, totals[b // PER_ROW])
    for b, total in enumerate(totals):
        edge[pl.ds(ROWS * b, ROWS), :] = total
    last_copy.wait()


def compact_rows(padded):
    return -(-padded // (ROWS * PER_ROW)) * ROWS


def pack(fields, flood, mix, ambient):
    levels = fields[0].shape[0]
    padded = (levels + 2 + ROWS - 1) // ROWS * ROWS
    return pl.pallas_call(
        functools.partial(pack_kernel, levels),
        out_shape=(
            jax.ShapeDtypeStruct((2, 4, padded, LANES), jnp.float32),
            jax.ShapeDtypeStruct((compact_rows(padded), LANES), jnp.float32),
            jax.ShapeDtypeStruct(ambient.shape, jnp.float32),
        ),
        in_specs=[pl.BlockSpec(memory_space=pltpu.HBM)] * 7,
        out_specs=(pl.BlockSpec(memory_space=pltpu.VMEM),) * 3,
        scratch_shapes=[
            pltpu.VMEM(flood.shape, flood.dtype),
            pltpu.VMEM(mix.shape, mix.dtype),
            pltpu.SemaphoreType.DMA((11,)),
        ],
        compiler_params=pltpu.CompilerParams(vmem_limit_bytes=VMEM_LIMIT),
    )(*[pltpu.with_memory_space_constraint(x, pltpu.HBM) for x in (*fields, flood, mix, ambient)])


def compact_place(b):
    return pl.ds(ROWS * (b // PER_ROW), ROWS), SPAN * (b % PER_ROW)


def widen_kernel(rounds, blocks, own, west, *messages):
    *messages, own_again = messages
    own_again[...] = own[...]
    lane = lax.broadcasted_iota(jnp.int32, (ROWS, LANES), 1)
    totals = [[jnp.zeros((ROWS, LANES), jnp.float32)] * (own.shape[0] // ROWS) for _ in messages]
    for b in range(blocks):
        rows, start = compact_place(b)
        line = pltpu.roll(own[rows, :], -start % LANES, 1)
        beside = pltpu.roll(west[rows, :], -start % LANES, 1)
        found = []
        for n in range(rounds):
            northward = lax.rem(lax.axis_index("lat") + n, 2) == 0
            pair = jnp.where(northward, line, pltpu.roll(line, LANES - 2, 1))
            corner = jnp.where(northward, pltpu.roll(beside, LANES - 3, 1), pltpu.roll(beside, LANES - 4, 1))
            found.append(jnp.where((lane & 2) == 0, pair, corner))
        found.append(jnp.where((lane & 2) == 0, line, pltpu.roll(beside, 2, 1)))
        for total, values in zip(totals, found):
            moved = pltpu.roll(values, start, 1)
            total[b // PER_ROW] = jnp.where((lane >> 5) == b % PER_ROW, moved, total[b // PER_ROW])
    for message, total in zip(messages, totals):
        for b, values in enumerate(total):
            message[pl.ds(ROWS * b, ROWS), :] = values


def widen(rounds, blocks, edge, west):
    vmem = pl.BlockSpec(memory_space=pltpu.VMEM)
    return pl.pallas_call(
        functools.partial(widen_kernel, rounds, blocks),
        out_shape=(jax.ShapeDtypeStruct(edge.shape, jnp.float32),) * (rounds + 2),
        in_specs=[vmem] * 2,
        out_specs=(vmem,) * (rounds + 2),
        compiler_params=pltpu.CompilerParams(vmem_limit_bytes=VMEM_LIMIT),
        cost_estimate=pl.CostEstimate(flops=WIDEN_COST, bytes_accessed=0, transcendentals=0),
    )(edge, west)


def edge_kernel(lat_count, south_east, north_east, fold, south, north, _, edges, lines):
    lat = lax.axis_index("lat")
    blocks = edges.shape[2] // ROWS
    lane = lax.broadcasted_iota(jnp.int32, (ROWS, LANES), 1)
    first_slot = (lane & 4) == 0

    def back(x, lanes):
        return pltpu.roll(x, -lanes % LANES, 1)

    def unpacked(ref, b, lanes=0):
        rows, start = compact_place(b)
        return back(ref[rows, :], start + lanes)

    def corners(b, beside, east, lanes):
        return jnp.where(first_slot, unpacked(beside, b, lanes), unpacked(east, b, 2 * lanes - 6))

    def put(b, ones, twos, sides):
        rows = pl.ds(ROWS * b, ROWS)
        below = lat > 0
        cells = jnp.where(below, unpacked(south, b), 0.0)
        beside = jnp.where(below, corners(b, south, south_east, 1), 0.0)
        lines[0, rows, :] = jnp.where((lane & 3) == 1, cells, ones)
        lines[1, rows, :] = jnp.where((lane & 3) == 0, cells, twos)
        lines[2, rows, :] = jnp.where((lane & 3) == 1, beside, sides)

    @pl.when(lat < lat_count - 1)
    def _():
        for b in range(blocks):
            put(b, unpacked(north, b), unpacked(north, b, 2), corners(b, north, north_east, 2))

    @pl.when(lat == lat_count - 1)
    def _():
        turned = jnp.where(lane >= 16, -1.0, 1.0)
        turned_two = jnp.where((lane >= 15) & (lane < LANES - 1), -1.0, 1.0)
        for b in range(blocks):
            near, other = unpacked(fold, b, 1), unpacked(fold, b, 3)
            sides = jnp.where(first_slot, unpacked(fold, b, 5), unpacked(fold, b, -1))
            put(
                b,
                turned * jnp.where(first_slot, near, other),
                turned_two * jnp.where(first_slot, other, near),
                turned * sides,
            )

    for b in range(blocks):
        rows = pl.ds(ROWS * b, ROWS)
        for f in range(4):
            edges[0, f, rows, :] = back(lines[0, rows, :], 8 * f + 1)
            edges[1, f, rows, :] = back(lines[1, rows, :], 8 * f)
            edges[2, f, rows, :] = back(lines[2, rows, :], 8 * f + 1)


def stencil(levels, lat_count, statics):
    lat = lax.axis_index("lat")
    lane = lax.broadcasted_iota(jnp.int32, (ROWS, LANES), 1)
    row = lax.broadcasted_iota(jnp.int32, (ROWS, LANES), 0)
    first_lane = lane == 0
    last_lane = lane == LANES - 1
    slot_1_lane = (lane == 3) | (lane == 4)
    south_lane = (lane == 0) | (lane == 4)

    def swap(x):
        return jnp.where(slot_1_lane, pltpu.roll(x, 4, 1), pltpu.roll(x, LANES - 4, 1))

    def to_slot(x, slot):
        return x if slot == 0 else pltpu.roll(x, LANES - 4, 1)

    def northern(x, edge):
        return jnp.where(last_lane, edge, pltpu.roll(x, LANES - 1, 1))

    def southern(x, edge):
        return jnp.where(first_lane, edge, pltpu.roll(x, 1, 1))

    def ring(own_0, own_1):
        return jnp.where(slot_1_lane, pltpu.roll(own_1, 4, 1), own_0)

    def static_row(ref, index, which):
        line = ref[index + (pl.ds(levels + which, 1), slice(None))]
        return jnp.broadcast_to(line, (ROWS, LANES))

    def neighbours(get, name):
        if name == "rim":
            centre = get("rim")
            beside = ring(get("own0"), get("own1"))
            beyond = get("rim2")
            north_cell = jnp.where(south_lane, beside, beyond)
            south_cell = jnp.where(south_lane, beyond, beside)
            return swap(centre), get("corner"), north_cell, south_cell
        slot = int(name[-1])
        centre = get(name)
        if name.startswith("own"):
            inner, outer, edge = get("own%d" % (1 - slot)), get("near%d" % slot), get("rim")
        else:
            inner, outer, edge = get("own%d" % slot), get("far%d" % slot), get("corner")
        edge = to_slot(edge, slot)
        return inner, outer, northern(centre, edge), southern(centre, edge)

    cell_sets = ("own0", "own1", "near0", "near1", "rim")

    def hold(held, names):
        for name in names:
            n = cell_sets.index(name)
            flood_at = neighbours(lambda k: held[k][0], name)
            mix_at = neighbours(lambda k: held[k][1], name)
            statics[n, 0] = held[name][0]
            for m in range(4):
                statics[n, 1 + m] = jnp.minimum(held[name][0], flood_at[m])
                statics[n, 5 + m] = (0.5 * DT) * (held[name][1] + mix_at[m])

    total_rows = LANES * lat_count
    place = lat * LANES + lane
    rim_place = lat * LANES + jnp.where(south_lane, -1, LANES)

    def turning(index):
        index = jnp.where(index >= total_rows, 2 * total_rows - 1 - index, index)
        return DT * (0.2 + index.astype(jnp.float32) / total_rows)

    planet = {True: turning(rim_place), False: turning(place)}
    sigma_of = {
        "own0": 1.0,
        "near0": 1.0,
        "own1": -1.0,
        "near1": -1.0,
        "rim": jnp.where(slot_1_lane, -1.0, 1.0),
    }

    def running(x, carry):
        for step in (1, 2, 4):
            x = x + jnp.where(row >= step, pltpu.roll(x, step, 0), 0.0)
        x = x + carry
        return x, jnp.broadcast_to(x[ROWS - 1 :, :], (ROWS, LANES))

    def advance(name, level, fields, pressure):
        n = cell_sets.index(name)
        wet = level < statics[n, 0]
        weights = [jnp.where(level < statics[n, 1 + m], statics[n, 5 + m], 0.0) for m in range(4)]
        keep = jnp.where(wet, 1.0, 0.0)
        centre = keep - ((weights[0] + weights[1]) + (weights[2] + weights[3]))
        half = jnp.where(wet, 0.5 * DT, 0.0)
        along = half * sigma_of[name]
        flow_u, flow_v = fields[2][name], fields[3][name]
        drift_u = along * flow_u
        drift_v = half * flow_v
        inner, outer, north_w, south_w = (
            weights[0] - drift_u,
            weights[1] + drift_u,
            weights[2] - drift_v,
            weights[3] + drift_v,
        )
        out = []
        for f in range(4):
            cells = neighbours(lambda k, f=f: fields[f][k], name)
            value = centre * fields[f][name]
            value = value + ((inner * cells[0] + outer * cells[1]) + (north_w * cells[2] + south_w * cells[3]))
            out.append(value)
        cells = neighbours(lambda k: pressure[k], name)
        turn = keep * planet[name == "rim"]
        out[2] = out[2] + (turn * flow_v - (0.5 * along) * (cells[0] - cells[1]))
        out[3] = out[3] - (turn * flow_u + (0.5 * half) * (cells[2] - cells[3]))
        return out

    def whole(sources):
        return {name: [static_row(r, i, w) for w in (FLOOD_ROW, MIX_ROW)] for name, (r, i) in sources.items()}

    turn_lane = jnp.where(last_lane, -1.0, jnp.where(first_lane, 1.0, 0.0))
    return types.SimpleNamespace(
        row=row, cell_sets=cell_sets, to_slot=to_slot, running=running, advance=advance, hold=hold, whole=whole, turn_lane=turn_lane
    )


def tile_sources(own, east, west):
    return {
        "own0": (own, (0, 0)),
        "own1": (own, (1, 0)),
        "near0": (west, (1, 0)),
        "near1": (east, (0, 0)),
        "far0": (west, (0, 0)),
        "far1": (east, (1, 0)),
    }


def inner_kernel(levels, lat_count, own, east, west, partial, pressure_out, statics):
    use = stencil(levels, lat_count, statics)
    blocks = own.shape[2] // ROWS
    zero = jnp.zeros((ROWS, LANES), jnp.float32)
    beyond = {"rim": zero, "corner": zero}
    sources = tile_sources(own, east, west)
    held = use.whole(sources)
    held.update({name: (zero, zero) for name in beyond})
    names = use.cell_sets[:4]
    use.hold(held, names)
    carry = {name: zero for name in sources}
    for b in range(blocks):
        rows = pl.ds(ROWS * b, ROWS)
        level = (use.row + ROWS * b).astype(jnp.float32)
        fields = [{k: r[i[0], f, rows, :] for k, (r, i) in sources.items()} | beyond for f in range(4)]
        pressure = dict(beyond)
        for k in sources:
            pressure[k], carry[k] = use.running(density(fields[0][k], fields[1][k]), carry[k])
        for s in range(2):
            pressure_out[s, rows, :] = pressure["own%d" % s]
        for n, name in enumerate(names):
            for f, value in enumerate(use.advance(name, level, fields, pressure)):
                partial[n, f, rows, :] = value


def step_kernel(
    levels,
    lat_count,
    own,
    east,
    west,
    partial,
    own_pressure,
    edges,
    ambient,
    temp_out,
    salt_out,
    zonal_out,
    merid_out,
    statics,
    ends,
    columns,
    couple,
    state,
    ratio,
    sems,
):
    use = stencil(levels, lat_count, statics)
    row, cell_sets, running = use.row, use.cell_sets, use.running
    blocks = own.shape[2] // ROWS
    zero = jnp.zeros((ROWS, LANES), jnp.float32)
    sources = tile_sources(own, east, west)
    sources.update({"rim": (edges, (0, 0)), "rim2": (edges, (1, 0)), "corner": (edges, (2, 0))})
    held = use.whole(sources)
    use.hold(held, ("own0", "own1", "rim"))
    names = cell_sets[:4]
    edge_of = ("rim", "rim", "corner", "corner")
    at_end = use.turn_lane != 0.0
    for n, name in enumerate(names):
        flood, mix = [use.to_slot(x, n % 2) for x in held[edge_of[n]]]
        ends[n, 0] = held[name][0]
        ends[n, 1] = jnp.where(at_end, jnp.minimum(held[name][0], flood), 0.0)
        ends[n, 2] = (0.5 * DT) * (held[name][1] + mix)
    half_turn = (0.5 * DT) * use.turn_lane
    ambient_row = [jnp.broadcast_to(ambient[s : s + 1, :], (ROWS, LANES)) for s in range(2)]
    rim_sets = ("rim", "rim2", "corner")

    def block_body(b, carry):
        carry_1, carry_2, carry_3 = carry
        rows = pl.ds(pl.multiple_of(ROWS * b, ROWS), ROWS)
        level = (row + ROWS * b).astype(jnp.float32)
        fields = [{k: sources[k][0][sources[k][1][0], f, rows, :] for k in names + rim_sets} for f in range(4)]
        pressure = {"own%d" % s: own_pressure[s, rows, :] for s in range(2)}
        next_1 = []
        for k, c in zip(rim_sets, carry_1):
            pressure[k], c = running(density(fields[0][k], fields[1][k]), c)
            next_1.append(c)
        updated = {"rim": use.advance("rim", level, fields, pressure)}
        for n, name in enumerate(names):
            weight = jnp.where(level < ends[n, 1], ends[n, 2], 0.0)
            half = jnp.where(level < ends[n, 0], half_turn, 0.0)
            reach = weight + half * fields[3][name]
            out = []
            for f in range(4):
                beyond = use.to_slot(fields[f][edge_of[n]], n % 2)
                out.append(partial[n, f, rows, :] + (reach * beyond - weight * fields[f][name]))
            out[3] = out[3] + (0.5 * half) * use.to_slot(pressure[edge_of[n]], n % 2)
            updated[name] = out
        fields = [{name: updated[name][f] for name in cell_sets} for f in range(4)]
        pressure = {}
        next_2 = []
        for k, c in zip(cell_sets, carry_2):
            pressure[k], c = running(density(fields[0][k], fields[1][k]), c)
            next_2.append(c)
        next_3 = []
        for s in range(2):
            final = use.advance("own%d" % s, level, fields, pressure)
            dense = density(final[0], final[1])
            above = jnp.where(row == 0, carry_3[s], pltpu.roll(dense, 1, 0))
            next_3.append(jnp.broadcast_to(dense[ROWS - 1 :, :], (ROWS, LANES)))
            gate = (level < statics[s, 0]) & (level > 0.0)
            lower = ambient_row[s] * (0.2 + 1.0 / (1.0 + 10.0 * jnp.maximum(dense - above, 0.0)))
            lower = jnp.where(gate, lower, 0.0)
            for f in range(4):
                columns[rows, 2 * f + s, :] = final[f]
                couple[rows, 2 * f + s, :] = lower
        return tuple(next_1), tuple(next_2), tuple(next_3)

    lax.fori_loop(
        0, blocks, block_body, ((zero,) * len(rim_sets), (zero,) * len(cell_sets), (zero,) * 2), unroll=blocks
    )

    middle = levels // 2
    one = jnp.ones((ROWS, LANES), jnp.float32)
    chains = [
        {"levels": range(start, stop, step), "step": step, "top": one, "bottom": one, "value": zero, "before": zero}
        for start, stop, step in ((0, middle + 1, 1), (levels - 1, middle, -1))
    ]
    for n in range(middle + 1):
        for chain in chains:
            if n >= len(chain["levels"]):
                continue
            k = chain["levels"][n]
            ahead = couple[k + 1] if chain["step"] > 0 else couple[k]
            grown = chain["top"] + ahead * chain["bottom"]
            inverse = chain["bottom"] / grown
            chain["value"] = columns[k] * inverse + (chain["before"] * inverse) * chain["value"]
            chain["share"] = ahead * inverse
            state[k] = chain["value"]
            ratio[k] = chain["share"]
            chain["top"] = grown + ahead * chain["top"]
            chain["bottom"] = grown
            if n % RESCALE == RESCALE - 1:
                chain["top"], chain["bottom"] = chain["top"] * (1.0 / grown), jnp.ones_like(grown)
            chain["before"] = ahead
    upper, lower = chains
    middle_value = (upper["value"] + upper["share"] * lower["value"]) / (1.0 - upper["share"] * lower["share"])
    copies = []

    def send(start, stop, group):
        for f, out in enumerate((temp_out, salt_out, zonal_out, merid_out)):
            part = pl.ds(start, stop - start)
            copy = pltpu.make_async_copy(state.at[part, pl.ds(2 * f, 2), :], out.at[part], sems.at[4 * group + f])
            copy.start()
            copies.append(copy)

    state[middle] = middle_value
    above = below = middle_value
    quarter = middle // 2
    for n in range(1, levels - middle):
        if middle - n >= 0:
            above = state[middle - n] + ratio[middle - n] * above
            state[middle - n] = above
        below = state[middle + n] + ratio[middle + n] * below
        state[middle + n] = below
        if n == quarter:
            send(middle - quarter, middle + quarter + 1, 0)
    send(0, middle - quarter, 1)
    send(middle + quarter + 1, levels, 2)
    for copy in copies:
        copy.wait()


def lat_rounds(count):
    rounds = [[(i, i ^ 1) for i in range(count) if i ^ 1 < count]]
    if count > 2:
        rounds.append([(i, j) for i in range(1, count) for j in [i + 1 if i % 2 else i - 1] if j < count])
    return rounds


def shards(temp, salt, zonal, merid, flood, mix, ambient):
    levels = temp.shape[0]
    lon_count = lax.axis_size("lon")
    lat_count = lax.axis_size("lat")
    axes = ("lon", "lat")
    tile, edge, ambient = pack((temp, salt, zonal, merid), flood, mix, ambient)
    def joint(lon_pairs, lat_pairs):
        return [
            (i * lat_count + m, j * lat_count + n) for i, j in lon_pairs for m, n in lat_pairs
        ]

    same = [(i, i) for i in range(lon_count)]
    around = [(0, lon_count - 1), (lon_count - 1, 0)]
    eastward = [(i, (i + 1) % lon_count) for i in range(lon_count)]
    westward = [(j, i) for i, j in eastward]
    same = [(i, i) for i in range(lon_count)]
    mirror = [(i, lon_count - 1 - i) for i in range(lon_count)]
    edge_west = lax.ppermute(edge, "lon", eastward)
    west = lax.ppermute(tile, "lon", eastward)
    east = lax.ppermute(tile, "lon", westward)
    rounds = lat_rounds(lat_count)
    *bands, top_edge, edge = widen(len(rounds), tile.shape[2] // ROWS, edge, edge_west)
    got = [
        (lax.ppermute(band, axes, joint(same, lats)), lax.ppermute(edge, axes, joint(westward, lats)))
        for band, lats in zip(bands, rounds)
    ]
    chip = [(i, i ^ 1) for i in range(lon_count)]
    pairs = joint(mirror, [(lat_count - 1, lat_count - 1)]) + joint(chip, [(i, i) for i in range(lat_count - 1)])
    fold = lax.ppermute(top_edge, axes, pairs)
    if len(got) == 1:
        south = north = got[0]
    else:
        flip = lax.rem(lax.axis_index("lat"), 2) == 0
        north = [jnp.where(flip, x, y) for x, y in zip(*got)]
        south = [jnp.where(flip, y, x) for x, y in zip(*got)]
    padded = tile.shape[2]
    vmem = pl.BlockSpec(memory_space=pltpu.VMEM)
    partial, own_pressure = pl.pallas_call(
        functools.partial(inner_kernel, levels, lat_count),
        out_shape=(
            jax.ShapeDtypeStruct((4, 4, padded, LANES), jnp.float32),
            jax.ShapeDtypeStruct((2, padded, LANES), jnp.float32),
        ),
        in_specs=[vmem] * 3,
        out_specs=(vmem, vmem),
        scratch_shapes=[pltpu.VMEM((5, 9, ROWS, LANES), jnp.float32)],
        compiler_params=pltpu.CompilerParams(vmem_limit_bytes=VMEM_LIMIT),
        cost_estimate=pl.CostEstimate(flops=INNER_COST, bytes_accessed=0, transcendentals=0),
    )(tile, east, west)
    edges = pl.pallas_call(
        functools.partial(edge_kernel, lat_count),
        out_shape=jax.ShapeDtypeStruct((3, 4, padded, LANES), jnp.float32),
        in_specs=[vmem] * 5 + [pl.BlockSpec(memory_space=pl.ANY)],
        out_specs=vmem,
        scratch_shapes=[pltpu.VMEM((3, padded, LANES), jnp.float32)],
        compiler_params=pltpu.CompilerParams(vmem_limit_bytes=VMEM_LIMIT),
    )(south[1], north[1], fold, south[0], north[0], own_pressure)
    result = jax.ShapeDtypeStruct(temp.shape, jnp.float32)
    return pl.pallas_call(
        functools.partial(step_kernel, levels, lat_count),
        out_shape=(result,) * 4,
        in_specs=[vmem] * 7,
        out_specs=(pl.BlockSpec(memory_space=pltpu.HBM),) * 4,
        scratch_shapes=[
            pltpu.VMEM((5, 9, ROWS, LANES), jnp.float32),
            pltpu.VMEM((4, 3, ROWS, LANES), jnp.float32),
            pltpu.VMEM((padded, ROWS, LANES), jnp.float32),
            pltpu.VMEM((padded, ROWS, LANES), jnp.float32),
            pltpu.VMEM((levels, ROWS, LANES), jnp.float32),
            pltpu.VMEM((levels, ROWS, LANES), jnp.float32),
            pltpu.SemaphoreType.DMA((12,)),
        ],
        compiler_params=pltpu.CompilerParams(vmem_limit_bytes=VMEM_LIMIT),
    )(tile, east, west, partial, own_pressure, edges, ambient)


def solution(mesh):
    cube = P(None, "lon", "lat")
    plane = P("lon", "lat")
    return jax.shard_map(
        shards,
        mesh=mesh,
        in_specs=(cube,) * 4 + (plane,) * 3,
        out_specs=(cube,) * 4,
        check_vma=False,
    )
```

```python
import functools
import types

import jax
import jax.numpy as jnp
from jax import lax
from jax.experimental import pallas as pl
from jax.experimental.pallas import tpu as pltpu
from jax.sharding import PartitionSpec as P

SUBSTEPS = 2
DT = 0.05

LANES = 128
VMEM_LIMIT = 16 << 20
SPAN = 32
PER_ROW = LANES // SPAN
INNER_COST = 1 << 30
WIDEN_COST = 1 << 32
RESCALE = 16
ROWS = 8
FLOOD_ROW = 0
MIX_ROW = 1


def density(temp, salt):
    return temp * (0.03 * salt - 0.05 * temp - 0.2) + 0.8 * salt


def pack_kernel(levels, temp, salt, zonal, merid, flood, mix, ambient, tile, edge, ambient_here, flood_here, mix_here, sems):
    copies = [
        pltpu.make_async_copy(flood, flood_here, sems.at[8]),
        pltpu.make_async_copy(mix, mix_here, sems.at[9]),
    ]
    for copy in copies:
        copy.start()
    for f, field in enumerate((temp, salt, zonal, merid)):
        for c in range(2):
            copy = pltpu.make_async_copy(
                field.at[:, c, :], tile.at[c, f, pl.ds(0, levels), :], sems.at[2 * f + c]
            )
            copy.start()
            copies.append(copy)
    last_copy = pltpu.make_async_copy(ambient, ambient_here, sems.at[10])
    last_copy.start()
    padded = tile.shape[2]
    zero = jnp.zeros((padded - levels, LANES), jnp.float32)
    for f in range(4):
        for s in range(2):
            tile[s, f, pl.ds(levels, padded - levels), :] = zero
    for copy in copies[:2]:
        copy.wait()
    for c in range(2):
        tile[c, 0, pl.ds(levels + FLOOD_ROW, 1), :] = flood_here[pl.ds(c, 1), :].astype(jnp.float32)
        tile[c, 0, pl.ds(levels + MIX_ROW, 1), :] = mix_here[pl.ds(c, 1), :]
    lane = lax.broadcasted_iota(jnp.int32, (ROWS, LANES), 1)
    totals = [jnp.zeros((ROWS, LANES), jnp.float32)] * (edge.shape[0] // ROWS)
    for f in range(4):
        for copy in copies[2 + 2 * f : 4 + 2 * f]:
            copy.wait()
        for s in range(2):
            for b in range(padded // ROWS):
                place = SPAN * (b % PER_ROW) + 8 * f + 4 * s
                moved = pltpu.roll(tile[s, f, pl.ds(ROWS * b, ROWS), :], (place + 2) % LANES, 1)
                totals[b // PER_ROW] = jnp.where((lane >> 2) == place // 4, moved, totals[b // PER_ROW])
    for b, total in enumerate(totals):
        edge[pl.ds(ROWS * b, ROWS), :] = total
    last_copy.wait()


def compact_rows(padded):
    return -(-padded // (ROWS * PER_ROW)) * ROWS


def pack(fields, flood, mix, ambient):
    levels = fields[0].shape[0]
    padded = (levels + 2 + ROWS - 1) // ROWS * ROWS
    return pl.pallas_call(
        functools.partial(pack_kernel, levels),
        out_shape=(
            jax.ShapeDtypeStruct((2, 4, padded, LANES), jnp.float32),
            jax.ShapeDtypeStruct((compact_rows(padded), LANES), jnp.float32),
            jax.ShapeDtypeStruct(ambient.shape, jnp.float32),
        ),
        in_specs=[pl.BlockSpec(memory_space=pltpu.HBM)] * 7,
        out_specs=(pl.BlockSpec(memory_space=pltpu.VMEM),) * 3,
        scratch_shapes=[
            pltpu.VMEM(flood.shape, flood.dtype),
            pltpu.VMEM(mix.shape, mix.dtype),
            pltpu.SemaphoreType.DMA((11,)),
        ],
        compiler_params=pltpu.CompilerParams(vmem_limit_bytes=VMEM_LIMIT),
    )(*[pltpu.with_memory_space_constraint(x, pltpu.HBM) for x in (*fields, flood, mix, ambient)])


def compact_place(b):
    return pl.ds(ROWS * (b // PER_ROW), ROWS), SPAN * (b % PER_ROW)


def widen_kernel(rounds, blocks, own, west, *messages):
    *messages, own_again = messages
    own_again[...] = own[...]
    lane = lax.broadcasted_iota(jnp.int32, (ROWS, LANES), 1)
    totals = [[jnp.zeros((ROWS, LANES), jnp.float32)] * (own.shape[0] // ROWS) for _ in messages]
    for b in range(blocks):
        rows, start = compact_place(b)
        line = pltpu.roll(own[rows, :], -start % LANES, 1)
        beside = pltpu.roll(west[rows, :], -start % LANES, 1)
        found = []
        for n in range(rounds):
            northward = lax.rem(lax.axis_index("lat") + n, 2) == 0
            pair = jnp.where(northward, line, pltpu.roll(line, LANES - 2, 1))
            corner = jnp.where(northward, pltpu.roll(beside, LANES - 3, 1), pltpu.roll(beside, LANES - 4, 1))
            found.append(jnp.where((lane & 2) == 0, pair, corner))
        found.append(jnp.where((lane & 2) == 0, line, pltpu.roll(beside, 2, 1)))
        for total, values in zip(totals, found):
            moved = pltpu.roll(values, start, 1)
            total[b // PER_ROW] = jnp.where((lane >> 5) == b % PER_ROW, moved, total[b // PER_ROW])
    for message, total in zip(messages, totals):
        for b, values in enumerate(total):
            message[pl.ds(ROWS * b, ROWS), :] = values


def widen(rounds, blocks, edge, west):
    vmem = pl.BlockSpec(memory_space=pltpu.VMEM)
    return pl.pallas_call(
        functools.partial(widen_kernel, rounds, blocks),
        out_shape=(jax.ShapeDtypeStruct(edge.shape, jnp.float32),) * (rounds + 2),
        in_specs=[vmem] * 2,
        out_specs=(vmem,) * (rounds + 2),
        compiler_params=pltpu.CompilerParams(vmem_limit_bytes=VMEM_LIMIT),
        cost_estimate=pl.CostEstimate(flops=WIDEN_COST, bytes_accessed=0, transcendentals=0),
    )(edge, west)


def edge_kernel(lat_count, south_east, north_east, south, north, fold, _, edges, lines):
    lat = lax.axis_index("lat")
    blocks = edges.shape[2] // ROWS
    lane = lax.broadcasted_iota(jnp.int32, (ROWS, LANES), 1)
    first_slot = (lane & 4) == 0

    def back(x, lanes):
        return pltpu.roll(x, -lanes % LANES, 1)

    def unpacked(ref, b, lanes=0):
        rows, start = compact_place(b)
        return back(ref[rows, :], start + lanes)

    def corners(b, beside, east, lanes):
        return jnp.where(first_slot, unpacked(beside, b, lanes), unpacked(east, b, 2 * lanes - 6))

    def put(b, ones, twos, sides):
        rows = pl.ds(ROWS * b, ROWS)
        below = lat > 0
        cells = jnp.where(below, unpacked(south, b), 0.0)
        beside = jnp.where(below, corners(b, south, south_east, 1), 0.0)
        lines[0, rows, :] = jnp.where((lane & 3) == 1, cells, ones)
        lines[1, rows, :] = jnp.where((lane & 3) == 0, cells, twos)
        lines[2, rows, :] = jnp.where((lane & 3) == 1, beside, sides)

    @pl.when(lat < lat_count - 1)
    def _():
        for b in range(blocks):
            put(b, unpacked(north, b), unpacked(north, b, 2), corners(b, north, north_east, 2))

    @pl.when(lat == lat_count - 1)
    def _():
        turned = jnp.where(lane >= 16, -1.0, 1.0)
        turned_two = jnp.where((lane >= 15) & (lane < LANES - 1), -1.0, 1.0)
        for b in range(blocks):
            near, other = unpacked(fold, b, 1), unpacked(fold, b, 3)
            sides = jnp.where(first_slot, unpacked(fold, b, 5), unpacked(fold, b, -1))
            put(
                b,
                turned * jnp.where(first_slot, near, other),
                turned_two * jnp.where(first_slot, other, near),
                turned * sides,
            )

    for b in range(blocks):
        rows = pl.ds(ROWS * b, ROWS)
        for f in range(4):
            edges[0, f, rows, :] = back(lines[0, rows, :], 8 * f + 1)
            edges[1, f, rows, :] = back(lines[1, rows, :], 8 * f)
            edges[2, f, rows, :] = back(lines[2, rows, :], 8 * f + 1)


def stencil(levels, lat_count, statics):
    lat = lax.axis_index("lat")
    lane = lax.broadcasted_iota(jnp.int32, (ROWS, LANES), 1)
    row = lax.broadcasted_iota(jnp.int32, (ROWS, LANES), 0)
    first_lane = lane == 0
    last_lane = lane == LANES - 1
    slot_1_lane = (lane == 3) | (lane == 4)
    south_lane = (lane == 0) | (lane == 4)

    def swap(x):
        return jnp.where(slot_1_lane, pltpu.roll(x, 4, 1), pltpu.roll(x, LANES - 4, 1))

    def to_slot(x, slot):
        return x if slot == 0 else pltpu.roll(x, LANES - 4, 1)

    def northern(x, edge):
        return jnp.where(last_lane, edge, pltpu.roll(x, LANES - 1, 1))

    def southern(x, edge):
        return jnp.where(first_lane, edge, pltpu.roll(x, 1, 1))

    def ring(own_0, own_1):
        return jnp.where(slot_1_lane, pltpu.roll(own_1, 4, 1), own_0)

    def static_row(ref, index, which):
        line = ref[index + (pl.ds(levels + which, 1), slice(None))]
        return jnp.broadcast_to(line, (ROWS, LANES))

    def neighbours(get, name):
        if name == "rim":
            centre = get("rim")
            beside = ring(get("own0"), get("own1"))
            beyond = get("rim2")
            north_cell = jnp.where(south_lane, beside, beyond)
            south_cell = jnp.where(south_lane, beyond, beside)
            return swap(centre), get("corner"), north_cell, south_cell
        slot = int(name[-1])
        centre = get(name)
        if name.startswith("own"):
            inner, outer, edge = get("own%d" % (1 - slot)), get("near%d" % slot), get("rim")
        else:
            inner, outer, edge = get("own%d" % slot), get("far%d" % slot), get("corner")
        edge = to_slot(edge, slot)
        return inner, outer, northern(centre, edge), southern(centre, edge)

    cell_sets = ("own0", "own1", "near0", "near1", "rim")

    def hold(held, names):
        for name in names:
            n = cell_sets.index(name)
            flood_at = neighbours(lambda k: held[k][0], name)
            mix_at = neighbours(lambda k: held[k][1], name)
            statics[n, 0] = held[name][0]
            for m in range(4):
                statics[n, 1 + m] = jnp.minimum(held[name][0], flood_at[m])
                statics[n, 5 + m] = (0.5 * DT) * (held[name][1] + mix_at[m])

    total_rows = LANES * lat_count
    place = lat * LANES + lane
    rim_place = lat * LANES + jnp.where(south_lane, -1, LANES)

    def turning(index):
        index = jnp.where(index >= total_rows, 2 * total_rows - 1 - index, index)
        return DT * (0.2 + index.astype(jnp.float32) / total_rows)

    planet = {True: turning(rim_place), False: turning(place)}
    sigma_of = {
        "own0": 1.0,
        "near0": 1.0,
        "own1": -1.0,
        "near1": -1.0,
        "rim": jnp.where(slot_1_lane, -1.0, 1.0),
    }

    def running(x, carry):
        for step in (1, 2, 4):
            x = x + jnp.where(row >= step, pltpu.roll(x, step, 0), 0.0)
        x = x + carry
        return x, jnp.broadcast_to(x[ROWS - 1 :, :], (ROWS, LANES))

    def advance(name, level, fields, pressure):
        n = cell_sets.index(name)
        wet = level < statics[n, 0]
        weights = [jnp.where(level < statics[n, 1 + m], statics[n, 5 + m], 0.0) for m in range(4)]
        keep = jnp.where(wet, 1.0, 0.0)
        centre = keep - ((weights[0] + weights[1]) + (weights[2] + weights[3]))
        half = jnp.where(wet, 0.5 * DT, 0.0)
        along = half * sigma_of[name]
        flow_u, flow_v = fields[2][name], fields[3][name]
        drift_u = along * flow_u
        drift_v = half * flow_v
        inner, outer, north_w, south_w = (
            weights[0] - drift_u,
            weights[1] + drift_u,
            weights[2] - drift_v,
            weights[3] + drift_v,
        )
        out = []
        for f in range(4):
            cells = neighbours(lambda k, f=f: fields[f][k], name)
            value = centre * fields[f][name]
            value = value + ((inner * cells[0] + outer * cells[1]) + (north_w * cells[2] + south_w * cells[3]))
            out.append(value)
        cells = neighbours(lambda k: pressure[k], name)
        turn = keep * planet[name == "rim"]
        out[2] = out[2] + (turn * flow_v - (0.5 * along) * (cells[0] - cells[1]))
        out[3] = out[3] - (turn * flow_u + (0.5 * half) * (cells[2] - cells[3]))
        return out

    def whole(sources):
        return {name: [static_row(r, i, w) for w in (FLOOD_ROW, MIX_ROW)] for name, (r, i) in sources.items()}

    turn_lane = jnp.where(last_lane, -1.0, jnp.where(first_lane, 1.0, 0.0))
    return types.SimpleNamespace(
        row=row, cell_sets=cell_sets, to_slot=to_slot, running=running, advance=advance, hold=hold, whole=whole, turn_lane=turn_lane
    )


def tile_sources(own, east, west):
    return {
        "own0": (own, (0, 0)),
        "own1": (own, (1, 0)),
        "near0": (west, (1, 0)),
        "near1": (east, (0, 0)),
        "far0": (west, (0, 0)),
        "far1": (east, (1, 0)),
    }


def inner_kernel(levels, lat_count, own, east, west, partial, pressure_out, statics):
    use = stencil(levels, lat_count, statics)
    blocks = own.shape[2] // ROWS
    zero = jnp.zeros((ROWS, LANES), jnp.float32)
    beyond = {"rim": zero, "corner": zero}
    sources = tile_sources(own, east, west)
    held = use.whole(sources)
    held.update({name: (zero, zero) for name in beyond})
    names = use.cell_sets[:4]
    use.hold(held, names)
    carry = {name: zero for name in sources}
    for b in range(blocks):
        rows = pl.ds(ROWS * b, ROWS)
        level = (use.row + ROWS * b).astype(jnp.float32)
        fields = [{k: r[i[0], f, rows, :] for k, (r, i) in sources.items()} | beyond for f in range(4)]
        pressure = dict(beyond)
        for k in sources:
            pressure[k], carry[k] = use.running(density(fields[0][k], fields[1][k]), carry[k])
        for s in range(2):
            pressure_out[s, rows, :] = pressure["own%d" % s]
        for n, name in enumerate(names):
            for f, value in enumerate(use.advance(name, level, fields, pressure)):
                partial[n, f, rows, :] = value


def step_kernel(
    levels,
    lat_count,
    own,
    east,
    west,
    partial,
    own_pressure,
    edges,
    ambient,
    temp_out,
    salt_out,
    zonal_out,
    merid_out,
    statics,
    ends,
    columns,
    couple,
    state,
    ratio,
    sems,
):
    use = stencil(levels, lat_count, statics)
    row, cell_sets, running = use.row, use.cell_sets, use.running
    blocks = own.shape[2] // ROWS
    zero = jnp.zeros((ROWS, LANES), jnp.float32)
    sources = tile_sources(own, east, west)
    sources.update({"rim": (edges, (0, 0)), "rim2": (edges, (1, 0)), "corner": (edges, (2, 0))})
    held = use.whole(sources)
    use.hold(held, ("own0", "own1", "rim"))
    names = cell_sets[:4]
    edge_of = ("rim", "rim", "corner", "corner")
    at_end = use.turn_lane != 0.0
    for n, name in enumerate(names):
        flood, mix = [use.to_slot(x, n % 2) for x in held[edge_of[n]]]
        ends[n, 0] = held[name][0]
        ends[n, 1] = jnp.where(at_end, jnp.minimum(held[name][0], flood), 0.0)
        ends[n, 2] = (0.5 * DT) * (held[name][1] + mix)
    half_turn = (0.5 * DT) * use.turn_lane
    ambient_row = [jnp.broadcast_to(ambient[s : s + 1, :], (ROWS, LANES)) for s in range(2)]
    rim_sets = ("rim", "rim2", "corner")

    def block_body(b, carry):
        carry_1, carry_2, carry_3 = carry
        rows = pl.ds(pl.multiple_of(ROWS * b, ROWS), ROWS)
        level = (row + ROWS * b).astype(jnp.float32)
        fields = [{k: sources[k][0][sources[k][1][0], f, rows, :] for k in names + rim_sets} for f in range(4)]
        pressure = {"own%d" % s: own_pressure[s, rows, :] for s in range(2)}
        next_1 = []
        for k, c in zip(rim_sets, carry_1):
            pressure[k], c = running(density(fields[0][k], fields[1][k]), c)
            next_1.append(c)
        updated = {"rim": use.advance("rim", level, fields, pressure)}
        for n, name in enumerate(names):
            weight = jnp.where(level < ends[n, 1], ends[n, 2], 0.0)
            half = jnp.where(level < ends[n, 0], half_turn, 0.0)
            reach = weight + half * fields[3][name]
            out = []
            for f in range(4):
                beyond = use.to_slot(fields[f][edge_of[n]], n % 2)
                out.append(partial[n, f, rows, :] + (reach * beyond - weight * fields[f][name]))
            out[3] = out[3] + (0.5 * half) * use.to_slot(pressure[edge_of[n]], n % 2)
            updated[name] = out
        fields = [{name: updated[name][f] for name in cell_sets} for f in range(4)]
        pressure = {}
        next_2 = []
        for k, c in zip(cell_sets, carry_2):
            pressure[k], c = running(density(fields[0][k], fields[1][k]), c)
            next_2.append(c)
        next_3 = []
        for s in range(2):
            final = use.advance("own%d" % s, level, fields, pressure)
            dense = density(final[0], final[1])
            above = jnp.where(row == 0, carry_3[s], pltpu.roll(dense, 1, 0))
            next_3.append(jnp.broadcast_to(dense[ROWS - 1 :, :], (ROWS, LANES)))
            gate = (level < statics[s, 0]) & (level > 0.0)
            lower = ambient_row[s] * (0.2 + 1.0 / (1.0 + 10.0 * jnp.maximum(dense - above, 0.0)))
            lower = jnp.where(gate, lower, 0.0)
            for f in range(4):
                columns[rows, 2 * f + s, :] = final[f]
                couple[rows, 2 * f + s, :] = lower
        return tuple(next_1), tuple(next_2), tuple(next_3)

    lax.fori_loop(
        0, blocks, block_body, ((zero,) * len(rim_sets), (zero,) * len(cell_sets), (zero,) * 2), unroll=blocks
    )

    middle = levels // 2
    one = jnp.ones((ROWS, LANES), jnp.float32)
    chains = [
        {"levels": range(start, stop, step), "step": step, "top": one, "bottom": one, "value": zero, "before": zero}
        for start, stop, step in ((0, middle + 1, 1), (levels - 1, middle, -1))
    ]
    for n in range(middle + 1):
        for chain in chains:
            if n >= len(chain["levels"]):
                continue
            k = chain["levels"][n]
            ahead = couple[k + 1] if chain["step"] > 0 else couple[k]
            grown = chain["top"] + ahead * chain["bottom"]
            inverse = chain["bottom"] / grown
            chain["value"] = columns[k] * inverse + (chain["before"] * inverse) * chain["value"]
            chain["share"] = ahead * inverse
            state[k] = chain["value"]
            ratio[k] = chain["share"]
            chain["top"] = grown + ahead * chain["top"]
            chain["bottom"] = grown
            if n % RESCALE == RESCALE - 1:
                chain["top"], chain["bottom"] = chain["top"] * (1.0 / grown), jnp.ones_like(grown)
            chain["before"] = ahead
    upper, lower = chains
    middle_value = (upper["value"] + upper["share"] * lower["value"]) / (1.0 - upper["share"] * lower["share"])
    copies = []

    def send(start, stop, group):
        for f, out in enumerate((temp_out, salt_out, zonal_out, merid_out)):
            part = pl.ds(start, stop - start)
            copy = pltpu.make_async_copy(state.at[part, pl.ds(2 * f, 2), :], out.at[part], sems.at[4 * group + f])
            copy.start()
            copies.append(copy)

    state[middle] = middle_value
    above = below = middle_value
    quarter = middle // 2
    for n in range(1, levels - middle):
        if middle - n >= 0:
            above = state[middle - n] + ratio[middle - n] * above
            state[middle - n] = above
        below = state[middle + n] + ratio[middle + n] * below
        state[middle + n] = below
        if n == quarter:
            send(middle - quarter, middle + quarter + 1, 0)
    send(0, middle - quarter, 1)
    send(middle + quarter + 1, levels, 2)
    for copy in copies:
        copy.wait()


def lat_rounds(count):
    rounds = [[(i, i ^ 1) for i in range(count) if i ^ 1 < count]]
    if count > 2:
        rounds.append([(i, j) for i in range(1, count) for j in [i + 1 if i % 2 else i - 1] if j < count])
    return rounds


def shards(temp, salt, zonal, merid, flood, mix, ambient):
    levels = temp.shape[0]
    lon_count = lax.axis_size("lon")
    lat_count = lax.axis_size("lat")
    axes = ("lon", "lat")
    tile, edge, ambient = pack((temp, salt, zonal, merid), flood, mix, ambient)
    def joint(lon_pairs, lat_pairs):
        return [
            (i * lat_count + m, j * lat_count + n) for i, j in lon_pairs for m, n in lat_pairs
        ]

    same = [(i, i) for i in range(lon_count)]
    around = [(0, lon_count - 1), (lon_count - 1, 0)]
    eastward = [(i, (i + 1) % lon_count) for i in range(lon_count)]
    westward = [(j, i) for i, j in eastward]
    same = [(i, i) for i in range(lon_count)]
    mirror = [(i, lon_count - 1 - i) for i in range(lon_count)]
    edge_west = lax.ppermute(edge, "lon", eastward)
    west = lax.ppermute(tile, "lon", eastward)
    east = lax.ppermute(tile, "lon", westward)
    rounds = lat_rounds(lat_count)
    *bands, top_edge, edge = widen(len(rounds), tile.shape[2] // ROWS, edge, edge_west)
    got = [
        (lax.ppermute(band, axes, joint(same, lats)), lax.ppermute(edge, axes, joint(westward, lats)))
        for band, lats in zip(bands, rounds)
    ]
    chip = [(i, i ^ 1) for i in range(lon_count)]
    pairs = joint(mirror, [(lat_count - 1, lat_count - 1)]) + joint(chip, [(i, i) for i in range(lat_count - 1)])
    fold = lax.ppermute(top_edge, axes, pairs)
    if len(got) == 1:
        south = north = got[0]
    else:
        flip = lax.rem(lax.axis_index("lat"), 2) == 0
        north = [jnp.where(flip, x, y) for x, y in zip(*got)]
        south = [jnp.where(flip, y, x) for x, y in zip(*got)]
    padded = tile.shape[2]
    vmem = pl.BlockSpec(memory_space=pltpu.VMEM)
    partial, own_pressure = pl.pallas_call(
        functools.partial(inner_kernel, levels, lat_count),
        out_shape=(
            jax.ShapeDtypeStruct((4, 4, padded, LANES), jnp.float32),
            jax.ShapeDtypeStruct((2, padded, LANES), jnp.float32),
        ),
        in_specs=[vmem] * 3,
        out_specs=(vmem, vmem),
        scratch_shapes=[pltpu.VMEM((5, 9, ROWS, LANES), jnp.float32)],
        compiler_params=pltpu.CompilerParams(vmem_limit_bytes=VMEM_LIMIT),
        cost_estimate=pl.CostEstimate(flops=INNER_COST, bytes_accessed=0, transcendentals=0),
    )(tile, east, west)
    edges = pl.pallas_call(
        functools.partial(edge_kernel, lat_count),
        out_shape=jax.ShapeDtypeStruct((3, 4, padded, LANES), jnp.float32),
        in_specs=[vmem] * 5 + [pl.BlockSpec(memory_space=pl.ANY)],
        out_specs=vmem,
        scratch_shapes=[pltpu.VMEM((3, padded, LANES), jnp.float32)],
        compiler_params=pltpu.CompilerParams(vmem_limit_bytes=VMEM_LIMIT),
    )(south[1], north[1], south[0], north[0], fold, own_pressure)
    result = jax.ShapeDtypeStruct(temp.shape, jnp.float32)
    return pl.pallas_call(
        functools.partial(step_kernel, levels, lat_count),
        out_shape=(result,) * 4,
        in_specs=[vmem] * 7,
        out_specs=(pl.BlockSpec(memory_space=pltpu.HBM),) * 4,
        scratch_shapes=[
            pltpu.VMEM((5, 9, ROWS, LANES), jnp.float32),
            pltpu.VMEM((4, 3, ROWS, LANES), jnp.float32),
            pltpu.VMEM((padded, ROWS, LANES), jnp.float32),
            pltpu.VMEM((padded, ROWS, LANES), jnp.float32),
            pltpu.VMEM((levels, ROWS, LANES), jnp.float32),
            pltpu.VMEM((levels, ROWS, LANES), jnp.float32),
            pltpu.SemaphoreType.DMA((12,)),
        ],
        compiler_params=pltpu.CompilerParams(vmem_limit_bytes=VMEM_LIMIT),
    )(tile, east, west, partial, own_pressure, edges, ambient)


def solution(mesh):
    cube = P(None, "lon", "lat")
    plane = P("lon", "lat")
    return jax.shard_map(
        shards,
        mesh=mesh,
        in_specs=(cube,) * 4 + (plane,) * 3,
        out_specs=(cube,) * 4,
        check_vma=False,
    )
```
